512 devices in a mesh: lat: 16 (over y, z_hi, core), lon: 32 (over x, z_lo).
Axes of the slice: x: 4, y: 4, z: 16 (z_hi: 2, z_lo: 8; z = z_hi * 8 + z_lo), core: 2. Of those that a mesh axis runs over, the one named last changes fastest.
Arguments:
- queries: bfloat16 [48, 1440, 1024], P('lat', 'lon'), may hold values from -68 to 68
- keys: bfloat16 [48, 1440, 1024], P('lat', 'lon'), may hold values from -6 to 6
- values: bfloat16 [48, 1440, 1024], P('lat', 'lon'), may hold values from -6 to 6
- cotangent: bfloat16 [48, 1440, 1024], P('lat', 'lon'), may hold values from -6 to 6
- pair_list: int32 [48, 9], replicated, may hold values from -1 to 8, as said below
- quad_index: int32 [48], replicated, may hold values from 0 to 31
- quad_table: float32 [32], replicated, may hold values from 0.1 to 1
Outputs:
- attended: bfloat16 [48, 1440, 1024], P('lat', 'lon')
- grad_queries: bfloat16 [48, 1440, 1024], P('lat', 'lon')
- grad_keys: bfloat16 [48, 1440, 1024], P('lat', 'lon')
- grad_values: bfloat16 [48, 1440, 1024], P('lat', 'lon')
The draws below stay inside these ranges and needn't reach their ends.
Inputs may be any that keep to these rules, and one draw needn't show every extreme that they name: `pair_list`: row r lists distinct codes in increasing order, then -1 in the remaining slots; code 4 (the query tile itself) is always listed, codes 1 and 7 are listed wherever the row they name lies inside 0 to 47, and no listed code names a row outside 0 to 47.
All inputs are finite; a program needn't handle non-finite values.
Results may differ from the reference program's by a relative error of at most 0.012.
The reference program's roundings to bfloat16 on the way count: a program that leaves them out, or rounds other values in their place, can miss the bound.
Values may be sent and summed in bfloat16 or wider, within the bound.
A program may use at most 64 MiB of HBM per device.

```python
import math
import jax
import jax.numpy as jnp
from jax import lax

HEADS = 16
HEAD = 64
D = 1024
TILE = 45
NPAIR = 9
QTAB = 32
NLAT = 48
NLON = 1440


def query_key_pair(key):
    shape_full = (NLAT, NLON, D)
    base_queries = jnp.clip(jax.random.normal(jax.random.fold_in(key, 11), shape_full, jnp.float32), -6.0, 6.0)
    base_keys = jnp.clip(jax.random.normal(jax.random.fold_in(key, 12), shape_full, jnp.float32), -6.0, 6.0)
    return (base_queries, base_keys)


def draw_queries(key, part):
    return query_key_pair(key)[0].astype(jnp.bfloat16)


def draw_keys(key, part):
    return query_key_pair(key)[1].astype(jnp.bfloat16)


def draw_pair_list(key, part):
    row_ids = jnp.arange(NLAT, dtype=jnp.int32)[:, None]
    code_ids = jnp.arange(NPAIR, dtype=jnp.int32)[None, :]
    chance = jax.random.randint(jax.random.fold_in(key, 21), (NLAT, NPAIR), 0, NLAT)
    chosen = (chance <= row_ids) | (code_ids == 4) | (code_ids == 1) | (code_ids == 7) | (row_ids == NLAT - 2)
    source = row_ids + code_ids // 3 - 1
    chosen = chosen & (source >= 0) & (source < NLAT)
    ordered = jnp.sort(jnp.where(chosen, code_ids, code_ids + 100), axis=1)
    return jnp.where(ordered < 100, ordered, -1).astype(jnp.int32)


def set_ends(values, rng, least, top_value):
    shape = values.shape
    place = [jax.random.randint(jax.random.fold_in(rng, axis), (), 0, shape[axis]) for axis in range(len(shape))]
    values = values.at[tuple(place)].set(least)
    longest = shape.index(max(shape))
    place[longest] = (place[longest] + 1) % shape[longest]
    return values.at[tuple(place)].set(top_value)


def steps_of(key, shape, shards, least, top_value):
    level, own = 1.0, jax.random.fold_in(key, 6)
    for axis_at, parts in shards:
        steps = jnp.exp(jax.random.uniform(jax.random.fold_in(own, axis_at), (parts,), jnp.float32, least / len(shards), top_value / len(shards)))
        level = level * jnp.repeat(steps, shape[axis_at] // parts).reshape([-1 if axis == axis_at else 1 for axis in range(len(shape))])
    return level


def centred(own_key, extent, width, most, split=(), held_as=jnp.bfloat16):
    level = steps_of(own_key, extent, split, -0.22, 0.18) if split else 1.0
    array = jax.random.normal(own_key, extent, jnp.float32) * width * level
    return jnp.minimum(jnp.maximum(array, -most), most).astype(held_as)


def setup_inputs(seed: int = 0) -> dict:
    key_list = jax.random.split(jax.random.key(seed), 8)
    return {
        "queries": draw_queries(jax.random.fold_in(key_list[7], 71), 0),
        "keys": draw_keys(jax.random.fold_in(key_list[7], 71), 0),
        "values": centred(key_list[2], (NLAT, NLON, D), 1.0, 6.0, ((0, 16), (1, 32))),
        "cotangent": centred(key_list[3], (NLAT, NLON, D), 1.0, 6.0, ((0, 16), (1, 32))),
        "pair_list": draw_pair_list(jax.random.fold_in(key_list[7], 71), 0),
        "quad_index": set_ends(jax.random.randint(key_list[5], (NLAT,), 0, QTAB), jax.random.fold_in(key_list[5], 1), 0, QTAB - 1).astype(jnp.int32),
        "quad_table": jnp.clip(jnp.exp(jax.random.uniform(key_list[6], (QTAB,), jnp.float32, math.log(0.1), math.log(1.0))), 0.1, 1.0),
    }


def rounded(float_values):
    return lax.optimization_barrier(float_values.astype(jnp.bfloat16)).astype(jnp.float32)

def reference(queries, keys, values, cotangent, pair_list, quad_index, quad_table):
    lat_count, lon_count, model_width = queries.shape
    tile_count = lon_count // TILE
    head_scale = HEAD ** (-0.5)
    shape_tiles = (lat_count, tile_count, TILE, HEADS, HEAD)
    q_tiles = queries.reshape(shape_tiles)
    k_tiles = keys.reshape(shape_tiles)
    v_tiles = values.reshape(shape_tiles)
    g_tiles = cotangent.reshape(shape_tiles)
    codes_all = jnp.arange(NPAIR, dtype=jnp.int32)
    lat_step = codes_all // 3 - 1
    lon_step = codes_all % 3 - 1
    member = jnp.any(pair_list[:, :, None] == codes_all[None, None, :], axis=1)
    row_weight = quad_table[quad_index]

    def gather_keys(tile_id):
        row_index = tile_id // tile_count
        col_index = tile_id % tile_count
        key_rows = jnp.clip(row_index + lat_step, 0, lat_count - 1).astype(jnp.int32)
        key_cols = ((col_index + lon_step) % tile_count).astype(jnp.int32)
        listed = member[row_index]
        weight = row_weight[key_rows]
        key_tile = k_tiles[key_rows, key_cols].astype(jnp.float32)
        value_tile = v_tiles[key_rows, key_cols].astype(jnp.float32)
        query_tile = q_tiles[row_index, col_index].astype(jnp.float32)
        grad_tile = g_tiles[row_index, col_index].astype(jnp.float32)
        return (listed, weight, key_tile, value_tile, query_tile, grad_tile)

    def forward_tile(tile_id):
        listed, weight, key_tile, value_tile, query_tile, grad_tile = gather_keys(tile_id)
        scores = jnp.einsum('qhd,ckhd->hqck', query_tile, key_tile) * head_scale
        pair_mask = listed[None, None, :, None]
        row_max = lax.optimization_barrier(jnp.max(jnp.where(pair_mask, scores, -1e+30), axis=(2, 3)))
        shares = jnp.where(pair_mask, weight[None, None, :, None] * jnp.exp(scores - row_max[:, :, None, None]), 0.0)
        row_total = lax.optimization_barrier(jnp.sum(shares, axis=(2, 3)))
        mixed_heads = jnp.einsum('hqck,ckhd->qhd', rounded(shares), value_tile) / row_total.T[:, :, None]
        attended_tile = mixed_heads.reshape(TILE, model_width).astype(jnp.bfloat16)
        attended_heads = attended_tile.astype(jnp.float32).reshape(TILE, HEADS, HEAD)
        row_delta = lax.optimization_barrier(jnp.sum(grad_tile * attended_heads, axis=-1)).T
        return (attended_tile, row_max + jnp.log(row_total), row_delta)
    tile_ids = jnp.arange(lat_count * tile_count, dtype=jnp.int32)
    attended, lse_all, delta_all = lax.map(forward_tile, tile_ids)

    def query_grad(tile_id):
        listed, weight, key_tile, value_tile, query_tile, grad_tile = gather_keys(tile_id)
        scores = jnp.einsum('qhd,ckhd->hqck', query_tile, key_tile) * head_scale
        pair_mask = listed[None, None, :, None]
        probs = jnp.where(pair_mask, weight[None, None, :, None] * jnp.exp(scores - lse_all[tile_id][:, :, None, None]), 0.0)
        grad_probs = jnp.einsum('qhd,ckhd->hqck', grad_tile, value_tile)
        slopes = rounded(probs * (grad_probs - delta_all[tile_id][:, :, None, None]))
        result = jnp.einsum('hqck,ckhd->qhd', slopes, key_tile) * head_scale
        return result.reshape(TILE, model_width).astype(jnp.bfloat16)
    grad_queries = lax.map(query_grad, tile_ids)

    def key_grad(tile_id):
        row_index = tile_id // tile_count
        col_index = tile_id % tile_count
        source_rows = row_index - lat_step
        inside = (source_rows >= 0) & (source_rows < lat_count)
        clipped = jnp.clip(source_rows, 0, lat_count - 1).astype(jnp.int32)
        source_cols = ((col_index - lon_step) % tile_count).astype(jnp.int32)
        listed = inside & member[clipped, codes_all]
        source_ids = (clipped * tile_count + source_cols).astype(jnp.int32)
        query_tile = q_tiles[clipped, source_cols].astype(jnp.float32)
        grad_tile = g_tiles[clipped, source_cols].astype(jnp.float32)
        lse_source = jnp.transpose(lse_all[source_ids], (1, 0, 2))
        delta_source = jnp.transpose(delta_all[source_ids], (1, 0, 2))
        key_tile = k_tiles[row_index, col_index].astype(jnp.float32)
        value_tile = v_tiles[row_index, col_index].astype(jnp.float32)
        weight = row_weight[row_index]
        scores = jnp.einsum('cqhd,khd->hcqk', query_tile, key_tile) * head_scale
        pair_mask = listed[None, :, None, None]
        probs = jnp.where(pair_mask, weight * jnp.exp(scores - lse_source[..., None]), 0.0)
        grad_probs = jnp.einsum('cqhd,khd->hcqk', grad_tile, value_tile)
        slopes = rounded(probs * (grad_probs - delta_source[..., None]))
        key_out = jnp.einsum('hcqk,cqhd->khd', slopes, query_tile) * head_scale
        value_out = jnp.einsum('hcqk,cqhd->khd', rounded(probs), grad_tile)
        return (key_out.reshape(TILE, model_width).astype(jnp.bfloat16), value_out.reshape(TILE, model_width).astype(jnp.bfloat16))
    grad_keys, grad_values = lax.map(key_grad, tile_ids)
    full_shape = (lat_count, lon_count, model_width)
    return (attended.reshape(full_shape), grad_queries.reshape(full_shape), grad_keys.reshape(full_shape), grad_values.reshape(full_shape))
```

```python
import jax
import jax.numpy as jnp
from jax import lax
from jax.experimental import pallas as pl
from jax.experimental.pallas import tpu as pltpu
from jax.sharding import PartitionSpec as P

HEADS = 16
HEAD = 64
TILE = 45
PAD = 48
NPAIR = 9
HALF = 512
GROUP = 256
STACK = 4 * PAD
SCALE = HEAD ** (-0.5)
MESH = pl.DeviceIdType.MESH
NT = (((1,), (1,)), ((), ()))


def dot_nt(a, b):
    return lax.dot_general(a, b, NT, preferred_element_type=jnp.float32)


def dot_nn(a, b):
    return jnp.dot(a, b, preferred_element_type=jnp.float32)


def stacked(tile):
    head = lax.broadcasted_iota(jnp.int32, (PAD, GROUP), 1) // HEAD
    return jnp.concatenate([jnp.where(head == h, tile, jnp.zeros_like(tile)) for h in range(4)], axis=0)


def unstacked(blocks):
    head = lax.broadcasted_iota(jnp.int32, (PAD, GROUP), 1) // HEAD
    out = blocks[0:PAD]
    for h in range(1, 4):
        out = jnp.where(head == h, blocks[h * PAD : (h + 1) * PAD], out)
    return out


def kernel(q_in, k_in, v_in, g_in, pair_ref, index_ref, table_ref, o_out, dq_out, dk_out, dv_out,
           stage, buf, stats, dk_acc, dv_acc, result, landed, ssem, rsem):
    lat_size, lon_size = lax.axis_size("lat"), lax.axis_size("lon")
    lat, lon = lax.axis_index("lat"), lax.axis_index("lon")
    bands = lat_size // 2
    rows = lat_size * 3
    core = lax.rem(lat, 2)
    band = lat // 2
    other = 1 - core
    east = lax.rem(lon + 1, lon_size)
    west = lax.rem(lon + lon_size - 1, lon_size)
    sides = (east, west)
    up = lax.rem(band + 1, bands)
    down = lax.rem(band + bands - 1, bands)
    toward = lax.rem(band + 2 * core - 1 + bands, bands)
    away = lax.rem(band + 1 - 2 * core + bands, bands)
    partner = (2 * band + other, lon)

    barrier = pltpu.get_barrier_semaphore()
    greeted = [partner]
    for side in sides:
        for h in range(2):
            greeted.append((2 * band + h, side))
    greeted += [(2 * toward, lon), (2 * toward + 1, lon), (2 * away + core, lon)]
    for device in greeted:
        pl.semaphore_signal(barrier, inc=1, device_id=device, device_id_type=MESH)

    mine = 1 + 3 * core

    def fill(pair, arrays):
        for a, ref in enumerate(arrays):
            for r in range(3):
                for h in range(2):
                    stage[pair, h, a, r, 32:PAD, :] = jnp.zeros((PAD - 32, HALF), jnp.bfloat16)
                    stage[pair, h, a, r, 0:TILE, :] = ref[r, :, h * HALF : (h + 1) * HALF]

    def own(pair):
        for a in range(2):
            for r in range(3):
                buf[pair, a, 1, mine + r] = stage[pair, core, a, r]

    def send(src, dst, s, r, device):
        return pltpu.make_async_remote_copy(
            src_ref=src, dst_ref=dst, send_sem=ssem.at[s], recv_sem=rsem.at[r],
            device_id=device, device_id_type=MESH)

    def arrive(dst, r):
        send(dst, dst, 0, r, partner).wait_recv()

    def partner_copy(p):
        return send(stage.at[p, other], buf.at[p, :, 1, pl.ds(mine, 3)], 11 * p, 11 * p, partner)

    def lat_copies(p):
        return [send(stage.at[p, h, :, 2 * core], buf.at[p, :, 1, 7 * other], 11 * p + 5 + h, 11 * p + 5 + core,
                     (2 * toward + h, lon)) for h in range(2)]

    def lon_copies(p):
        return [send(stage.at[p, h], buf.at[p, :, 2 * d, pl.ds(mine, 3)], 11 * p + 1 + 2 * d + h,
                     11 * p + 1 + 2 * d + core, (2 * band + h, sides[d])) for d in range(2) for h in range(2)]

    def corner_copies(p, e):
        return [send(buf.at[p, :, 1, 7 * e], buf.at[p, :, 2 * d, 7 * e], 11 * p + 7 + 2 * d + e,
                     11 * p + 7 + 2 * d + e, (lat, sides[d])) for d in range(2)]

    def partner_arrive(p):
        arrive(buf.at[p, :, 1, pl.ds(1 + 3 * other, 3)], 11 * p)

    def lat_arrive(p, e):
        arrive(buf.at[p, :, 1, 7 * e], 11 * p + 6 - e)

    def lon_arrive(p, d):
        for s in range(2):
            arrive(buf.at[p, :, 2 * d, pl.ds(1 + 3 * s, 3)], 11 * p + 1 + 2 * d + s)

    def corner_arrive(p, d, e):
        arrive(buf.at[p, :, 2 * d, 7 * e], 11 * p + 7 + 2 * d + e)

    def stats_lat(e):
        return send(stats.at[1, 6 - 5 * e], stats.at[1, 7 * e], 22 + e, 22 + e, (2 * (up, down)[e] + core, lon))

    def stats_lon(d):
        return send(stats.at[1, pl.ds(1, 6)], stats.at[2 * d, pl.ds(1, 6)], 24 + d, 24 + d, (lat, sides[d]))

    def stats_corner(d, e):
        return send(stats.at[1, 7 * e], stats.at[2 * d, 7 * e], 26 + 2 * d + e, 26 + 2 * d + e, (lat, sides[d]))

    def result_copy(i):
        return send(result.at[pl.ds(2 * i, 2), pl.ds(3 * other, 3)], landed.at[pl.ds(2 * i, 2)], 30 + i, 30 + i, partner)

    def global_row(r):
        return lax.rem(6 * band + r - 1 + rows, rows)

    def row_weight(r):
        return table_ref[index_ref[global_row(r)]]

    def listed(r, code):
        hit = pair_ref[global_row(r), 0] == code
        for s in range(1, NPAIR):
            hit = hit | (pair_ref[global_row(r), s] == code)
        return hit

    def query_side(r):
        at = lax.broadcasted_iota(jnp.int32, (1, 9 * PAD), 1)
        block = at // PAD
        a = lax.rem(block, 3)
        mask = listed(r, 3 * a + block // 3) & (lax.rem(at, PAD) < TILE)
        weight = jnp.where(a == 0, row_weight(r - 1), jnp.where(a == 1, row_weight(r), row_weight(r + 1)))
        eye = (lax.broadcasted_iota(jnp.int32, (STACK, STACK), 0)
               == lax.broadcasted_iota(jnp.int32, (STACK, STACK), 1))
        for g in range(2):
            lanes = slice(g * GROUP, (g + 1) * GROUP)
            keys = jnp.concatenate(
                [buf[0, 0, c, pl.ds(r - 1, 3), :, lanes].reshape(3 * PAD, GROUP) for c in range(3)], axis=0)
            values = jnp.concatenate(
                [buf[0, 1, c, pl.ds(r - 1, 3), :, lanes].reshape(3 * PAD, GROUP) for c in range(3)], axis=0)
            qm = stacked(buf[1, 0, 1, r, :, lanes])
            gm = stacked(buf[1, 1, 1, r, :, lanes])
            scores = jnp.where(mask, dot_nt(qm, keys) * SCALE, -1e30)
            row_max = jnp.max(scores, axis=1, keepdims=True)
            shares = weight * jnp.exp(scores - row_max)
            total = jnp.sum(shares, axis=1, keepdims=True)
            mixed = dot_nn(shares.astype(jnp.bfloat16), values) / total
            attended = unstacked(mixed).astype(jnp.bfloat16)
            attended4 = jnp.concatenate([attended] * 4, axis=0).astype(jnp.float32)
            delta = jnp.sum(gm.astype(jnp.float32) * attended4, axis=1, keepdims=True)
            lse = row_max + jnp.log(total)
            slopes = shares * (1.0 / total) * (dot_nt(gm, values) - delta)
            grad = dot_nn(slopes.astype(jnp.bfloat16), keys) * SCALE
            result[0, r - 1, :, lanes] = attended
            result[1, r - 1, :, lanes] = unstacked(grad).astype(jnp.bfloat16)
            stats[1, r, g : g + 1, 0:STACK] = jnp.sum(jnp.where(eye, lse, 0.0), axis=0, keepdims=True)
            stats[1, r, 2 + g : 3 + g, 0:STACK] = jnp.sum(jnp.where(eye, delta, 0.0), axis=0, keepdims=True)

    def key_side(c, r, first, count, a_first):
        at = lax.broadcasted_iota(jnp.int32, (count * PAD, 1), 0)
        a = a_first + at // PAD
        mask = listed(r, 3 * a + 2 - c) & (lax.rem(at, PAD) < TILE)
        weight = jnp.full((count * PAD, 1), row_weight(first), jnp.float32)
        for i in range(1, count):
            weight = jnp.where(at >= i * PAD, row_weight(first + i), weight)
        for g in range(2):
            lanes = slice(g * GROUP, (g + 1) * GROUP)
            keys = buf[0, 0, 1, pl.ds(first, count), :, lanes].reshape(count * PAD, GROUP)
            values = buf[0, 1, 1, pl.ds(first, count), :, lanes].reshape(count * PAD, GROUP)
            qm = stacked(buf[1, 0, c, r, :, lanes])
            gm = stacked(buf[1, 1, c, r, :, lanes])
            lse = stats[c, r, g : g + 1, 0:STACK]
            delta = stats[c, r, 2 + g : 3 + g, 0:STACK]
            probs = jnp.where(mask, weight * jnp.exp(dot_nt(keys, qm) * SCALE - lse), 0.0)
            slopes = probs * (dot_nt(values, gm) - delta)
            dv = dot_nn(probs.astype(jnp.bfloat16), gm)
            dk = dot_nn(slopes.astype(jnp.bfloat16), qm)
            dv_acc[pl.ds(first, count), :, lanes] += dv.reshape(count, PAD, GROUP)
            dk_acc[pl.ds(first, count), :, lanes] += dk.reshape(count, PAD, GROUP)

    def near(c, r):
        key_side(c, r, r - 1, 3, 0)

    def rim(c, e):
        key_side(c, 7 * e, 1 + 5 * e, 1, 2 - 2 * e)

    fill(0, (k_in, v_in))
    fill(1, (q_in, g_in))
    pl.semaphore_wait(barrier, len(greeted))
    sent = []

    def start(copies):
        for copy in copies:
            copy.start()
        sent.extend(copies)

    kv_lon = lon_copies(0)
    start(lat_copies(0))
    start([partner_copy(0), partner_copy(1)])
    for copy in kv_lon:
        copy.start()
    own(0)
    own(1)
    dk_acc[...] = jnp.zeros_like(dk_acc)
    dv_acc[...] = jnp.zeros_like(dv_acc)
    for e in range(2):
        lat_arrive(0, e)
        start(corner_copies(0, e))
    start(lat_copies(1))
    for copy in kv_lon:
        copy.wait_send()
    start(lon_copies(1))
    partner_arrive(0)
    partner_arrive(1)
    for d in range(2):
        lon_arrive(0, d)
        for e in range(2):
            corner_arrive(0, d, e)

    def query_step(i, carry):
        query_side(i + 1)
        return carry

    lax.fori_loop(0, 6, query_step, 0)
    start([stats_lat(0), stats_lat(1), stats_lon(0), stats_lon(1), result_copy(0)])

    def own_step(i, carry):
        near(1, i + 1)
        return carry

    lax.fori_loop(0, 6, own_step, 0)
    for e in range(2):
        arrive(stats.at[1, 7 * e], 22 + e)
        start([stats_corner(0, e), stats_corner(1, e)])
    for e in range(2):
        lat_arrive(1, e)
        start(corner_copies(1, e))

    def rim_step(e, carry):
        rim(1, e)
        return carry

    lax.fori_loop(0, 2, rim_step, 0)
    for d in range(2):
        arrive(stats.at[2 * d, pl.ds(1, 6)], 24 + d)
        lon_arrive(1, d)

    def side_step(i, carry):
        near(2 * (i // 6), 1 + lax.rem(i, 6))
        return carry

    lax.fori_loop(0, 12, side_step, 0)
    for d in range(2):
        for e in range(2):
            arrive(stats.at[2 * d, 7 * e], 26 + 2 * d + e)
            corner_arrive(1, d, e)

    def corner_step(i, carry):
        rim(2 * (i // 2), lax.rem(i, 2))
        return carry

    lax.fori_loop(0, 4, corner_step, 0)
    for r in range(6):
        result[2, r] = (dk_acc[r + 1] * SCALE).astype(jnp.bfloat16)
        result[3, r] = dv_acc[r + 1].astype(jnp.bfloat16)
    start([result_copy(1)])
    mine_lanes = pl.ds(pl.multiple_of(core * HALF, HALF), HALF)
    other_lanes = pl.ds(pl.multiple_of(other * HALF, HALF), HALF)
    outs = (o_out, dq_out, dk_out, dv_out)
    for i in range(2):
        arrive(landed.at[pl.ds(2 * i, 2)], 30 + i)
    for i, out in enumerate(outs):
        for r in range(3):
            out[r, :, mine_lanes] = result[i, 3 * core + r, 0:TILE, :]
            out[r, :, other_lanes] = landed[i, r, 0:TILE, :]
    for copy in sent:
        copy.wait_send()


def on_device(queries, keys, values, cotangent, pair_list, quad_index, quad_table):
    vmem = pl.BlockSpec(memory_space=pltpu.VMEM)
    smem = pl.BlockSpec(memory_space=pltpu.SMEM)
    return tuple(pl.pallas_call(
        kernel,
        out_shape=[jax.ShapeDtypeStruct(queries.shape, jnp.bfloat16)] * 4,
        in_specs=[vmem] * 4 + [smem] * 3,
        out_specs=[vmem] * 4,
        scratch_shapes=[
            pltpu.VMEM((2, 2, 2, 3, PAD, HALF), jnp.bfloat16),
            pltpu.VMEM((2, 2, 3, 8, PAD, HALF), jnp.bfloat16),
            pltpu.VMEM((3, 8, 8, 256), jnp.float32),
            pltpu.VMEM((8, PAD, HALF), jnp.float32),
            pltpu.VMEM((8, PAD, HALF), jnp.float32),
            pltpu.VMEM((4, 6, PAD, HALF), jnp.bfloat16),
            pltpu.VMEM((4, 3, PAD, HALF), jnp.bfloat16),
            pltpu.SemaphoreType.DMA((32,)),
            pltpu.SemaphoreType.DMA((32,)),
        ],
        compiler_params=pltpu.CompilerParams(
            collective_id=0, has_side_effects=True, vmem_limit_bytes=48 * 2**20),
        name="sphere",
    )(queries, keys, values, cotangent, pair_list, quad_index, quad_table))


def solution(mesh):
    grid = P("lat", "lon", None)
    return jax.shard_map(
        on_device, mesh=mesh, in_specs=(grid,) * 4 + (P(),) * 3, out_specs=(grid,) * 4, check_vma=False)
```

```python
import jax
import jax.numpy as jnp
from jax import lax
from jax.experimental import pallas as pl
from jax.experimental.pallas import tpu as pltpu
from jax.sharding import PartitionSpec as P

HEADS = 16
HEAD = 64
TILE = 45
PAD = 48
NPAIR = 9
RUN = 8
VMEM_BYTES = 64 * 2**20 - 2**17
HALF = 512
GROUP = 256
STACK = 4 * PAD
SCALE = HEAD ** (-0.5)
MESH = pl.DeviceIdType.MESH
NT = (((1,), (1,)), ((), ()))


def dot_nt(a, b):
    return lax.dot_general(a, b, NT, preferred_element_type=jnp.float32)


def dot_nn(a, b):
    return jnp.dot(a, b, preferred_element_type=jnp.float32)


def stacked(tile):
    head = lax.broadcasted_iota(jnp.int32, (PAD, GROUP), 1) // HEAD
    return jnp.concatenate([jnp.where(head == h, tile, jnp.zeros_like(tile)) for h in range(4)], axis=0)


def unstacked(blocks):
    head = lax.broadcasted_iota(jnp.int32, (PAD, GROUP), 1) // HEAD
    out = blocks[0:PAD]
    for h in range(1, 4):
        out = jnp.where(head == h, blocks[h * PAD : (h + 1) * PAD], out)
    return out


def kernel(q_in, k_in, v_in, g_in, pair_in, index_in, table_in, o_out, dq_out, dk_out, dv_out,
           made, loaded, stage, buf, stats, dk_acc, dv_acc, result, landed, pair_ref, index_ref, table_ref,
           lsem, ssem, rsem, row_ssem, row_rsem):
    lat_size, lon_size = lax.axis_size("lat"), lax.axis_size("lon")
    lat, lon = lax.axis_index("lat"), lax.axis_index("lon")
    bands = lat_size // 2
    rows = lat_size * 3
    core = lax.rem(lat, 2)
    band = lat // 2
    other = 1 - core
    east = lax.rem(lon + 1, lon_size)
    west = lax.rem(lon + lon_size - 1, lon_size)
    sides = (east, west)
    up = lax.rem(band + 1, bands)
    down = lax.rem(band + bands - 1, bands)
    toward = lax.rem(band + 2 * core - 1 + bands, bands)
    place = lax.rem(lon, RUN)
    partner = (2 * band + other, lon)

    barrier = pltpu.get_barrier_semaphore()
    greeted = [partner]
    greeted += [(2 * band + h, side) for side in sides for h in range(2)]
    greeted += [(2 * b + h, to) for b in (up, down) for to in (west, lon, east) for h in range(2)]
    for device in greeted:
        pl.semaphore_signal(barrier, inc=1, device_id=device, device_id_type=MESH)

    inputs = (k_in, v_in, q_in, g_in)
    loads = [pltpu.make_async_copy(ref, loaded.at[i], lsem.at[i]) for i, ref in enumerate(inputs)]
    small = [pltpu.make_async_copy(src, dst, lsem.at[4 + i]) for i, (src, dst) in enumerate(
        ((pair_in, pair_ref), (index_in, index_ref), (table_in, table_ref)))]
    for load in loads + small:
        load.start()

    mine = 1 + 3 * core

    def fill(pair):
        for a in range(2):
            loads[2 * pair + a].wait()
            for r in range(3):
                for h in range(2):
                    stage[pair, h, a, r, 32:PAD, :] = jnp.zeros((PAD - 32, HALF), jnp.bfloat16)
                    stage[pair, h, a, r, 0:TILE, :] = loaded[2 * pair + a, r, :, h * HALF : (h + 1) * HALF]

    def own(pair):
        for a in range(2):
            for r in range(3):
                buf[pair, a, 1, mine + r] = stage[pair, core, a, r]

    def send(src, dst, s, r, device):
        return pltpu.make_async_remote_copy(
            src_ref=src, dst_ref=dst, send_sem=ssem.at[s], recv_sem=rsem.at[r],
            device_id=device, device_id_type=MESH)

    def arrive(dst, r):
        send(dst, dst, 0, r, partner).wait_recv()

    def partner_copy(p):
        return send(stage.at[p, other], buf.at[p, :, 1, pl.ds(mine, 3)], 15 * p, 11 * p, partner)

    def lon_copies(p):
        return [send(stage.at[p, h], buf.at[p, :, 2 * d, pl.ds(mine, 3)], 15 * p + 1 + 2 * d + h,
                     11 * p + 1 + 2 * d + core, (2 * band + h, sides[d])) for d in range(2) for h in range(2)]

    def lon_rows():
        return [pltpu.make_async_remote_copy(
            src_ref=stage.at[1, h, :, r], dst_ref=buf.at[1, :, 2 * d, mine + r],
            send_sem=row_ssem.at[4 * r + 2 * d + h], recv_sem=row_rsem.at[4 * r + 2 * d + core],
            device_id=(2 * band + h, sides[d]), device_id_type=MESH)
            for r in range(3) for d in range(2) for h in range(2)]

    def slot(p, col, e):
        return buf.at[p, :, col, 7 * e]

    def seam_copies(p, number, col, to):
        return [send(stage.at[p, h, :, 2 * core], slot(p, col, other), 15 * p + number + h,
                     11 * p + 5 + 2 * col + other, (2 * toward + h, to)) for h in range(2)]

    def seam_near(p):
        return seam_copies(p, 5, 2 * core, core * west + other * east)

    def seam_same(p):
        return seam_copies(p, 7, 1, lon)

    def seam_far(p):
        return seam_copies(p, 9, 2 * other, core * east + other * west)

    def relay(p, e, step):
        col = (2 - step, step)[e]
        to = (1 - step, 1 + step)[e]
        return send(slot(p, col, e), slot(p, to, e), 15 * p + 11 + 2 * step + e, 11 * p + 5 + 2 * to + e,
                    (lat, sides[e]))

    same_when = place == (RUN - 1) * other
    far_when = place == (RUN - 1) * core
    relay_when = (place != RUN - 1, place != 0)

    def seam_start(p):
        for copy in seam_near(p):
            copy.start()

        @pl.when(same_when)
        def _():
            for copy in seam_same(p):
                copy.start()

        @pl.when(far_when)
        def _():
            for copy in seam_far(p):
                copy.start()

    def seam_sent(p):
        for copy in seam_near(p):
            copy.wait_send()

        @pl.when(same_when)
        def _():
            for copy in seam_same(p):
                copy.wait_send()

        @pl.when(far_when)
        def _():
            for copy in seam_far(p):
                copy.wait_send()

    def relay_start(p, step):
        for e in range(2):
            slot_arrive(p, ((2, 0), (1, 1))[step][e], e)

            @pl.when(relay_when[e])
            def _():
                relay(p, e, step).start()

    def relay_sent(p, step):
        for e in range(2):

            @pl.when(relay_when[e])
            def _():
                relay(p, e, step).wait_send()

    def slot_arrive(p, col, e):
        arrive(slot(p, col, e), 11 * p + 5 + 2 * col + e)

    def partner_arrive(p):
        arrive(buf.at[p, :, 1, pl.ds(1 + 3 * other, 3)], 11 * p)

    def lon_arrive(p, d):
        for s in range(2):
            arrive(buf.at[p, :, 2 * d, pl.ds(1 + 3 * s, 3)], 11 * p + 1 + 2 * d + s)

    def stats_lat(e):
        return send(stats.at[1, 6 - 5 * e], stats.at[1, 7 * e], 30 + e, 22 + e, (2 * (up, down)[e] + core, lon))

    def stats_lon(d):
        return send(stats.at[1, pl.ds(1, 6)], stats.at[2 * d, pl.ds(1, 6)], 32 + d, 24 + d, (lat, sides[d]))

    def stats_corner(d, e):
        return send(stats.at[1, 7 * e], stats.at[2 * d, 7 * e], 34 + 2 * d + e, 26 + 2 * d + e, (lat, sides[d]))

    def result_copy(i):
        return send(result.at[pl.ds(2 * i, 2), pl.ds(3 * other, 3)], landed.at[pl.ds(2 * i, 2)], 38 + i, 30 + i, partner)

    def global_row(r):
        return lax.rem(6 * band + r - 1 + rows, rows)

    def row_weight(r):
        return table_ref[index_ref[global_row(r)]]

    def listed(r, code):
        hit = pair_ref[0, global_row(r)] == code
        for s in range(1, NPAIR):
            hit = hit | (pair_ref[s, global_row(r)] == code)
        return hit

    def query_side(r):
        at = lax.broadcasted_iota(jnp.int32, (1, 9 * PAD), 1)
        block = at // PAD
        a = lax.rem(block, 3)
        mask = listed(r, 3 * a + block // 3) & (lax.rem(at, PAD) < TILE)
        weight = jnp.where(a == 0, row_weight(r - 1), jnp.where(a == 1, row_weight(r), row_weight(r + 1)))
        eye = (lax.broadcasted_iota(jnp.int32, (STACK, STACK), 0)
               == lax.broadcasted_iota(jnp.int32, (STACK, STACK), 1))
        for g in range(2):
            lanes = slice(g * GROUP, (g + 1) * GROUP)
            keys = jnp.concatenate(
                [buf[0, 0, c, pl.ds(r - 1, 3), :, lanes].reshape(3 * PAD, GROUP) for c in range(3)], axis=0)
            values = jnp.concatenate(
                [buf[0, 1, c, pl.ds(r - 1, 3), :, lanes].reshape(3 * PAD, GROUP) for c in range(3)], axis=0)
            qm = stacked(buf[1, 0, 1, r, :, lanes])
            gm = stacked(buf[1, 1, 1, r, :, lanes])
            scores = jnp.where(mask, dot_nt(qm, keys) * SCALE, -1e30)
            row_max = jnp.max(scores, axis=1, keepdims=True)
            shares = weight * jnp.exp(scores - row_max)
            total = jnp.sum(shares, axis=1, keepdims=True)
            mixed = dot_nn(shares.astype(jnp.bfloat16), values) / total
            attended = unstacked(mixed).astype(jnp.bfloat16)
            attended4 = jnp.concatenate([attended] * 4, axis=0).astype(jnp.float32)
            delta = jnp.sum(gm.astype(jnp.float32) * attended4, axis=1, keepdims=True)
            lse = row_max + jnp.log(total)
            slopes = shares * (1.0 / total) * (dot_nt(gm, values) - delta)
            grad = dot_nn(slopes.astype(jnp.bfloat16), keys) * SCALE
            result[0, r - 1, :, lanes] = attended
            result[1, r - 1, :, lanes] = unstacked(grad).astype(jnp.bfloat16)
            stats[1, r, g : g + 1, 0:STACK] = jnp.sum(jnp.where(eye, lse, 0.0), axis=0, keepdims=True)
            stats[1, r, 2 + g : 3 + g, 0:STACK] = jnp.sum(jnp.where(eye, delta, 0.0), axis=0, keepdims=True)

    def key_side(c, r, first, count, a_first):
        at = lax.broadcasted_iota(jnp.int32, (count * PAD, 1), 0)
        a = a_first + at // PAD
        mask = listed(r, 3 * a + 2 - c) & (lax.rem(at, PAD) < TILE)
        weight = jnp.full((count * PAD, 1), row_weight(first), jnp.float32)
        for i in range(1, count):
            weight = jnp.where(at >= i * PAD, row_weight(first + i), weight)
        for g in range(2):
            lanes = slice(g * GROUP, (g + 1) * GROUP)
            keys = buf[0, 0, 1, pl.ds(first, count), :, lanes].reshape(count * PAD, GROUP)
            values = buf[0, 1, 1, pl.ds(first, count), :, lanes].reshape(count * PAD, GROUP)
            qm = stacked(buf[1, 0, c, r, :, lanes])
            gm = stacked(buf[1, 1, c, r, :, lanes])
            lse = stats[c, r, g : g + 1, 0:STACK]
            delta = stats[c, r, 2 + g : 3 + g, 0:STACK]
            probs = jnp.where(mask, weight * jnp.exp(dot_nt(keys, qm) * SCALE - lse), 0.0)
            slopes = probs * (dot_nt(values, gm) - delta)
            dv = dot_nn(probs.astype(jnp.bfloat16), gm)
            dk = dot_nn(slopes.astype(jnp.bfloat16), qm)
            dv_acc[pl.ds(first, count), :, lanes] += dv.reshape(count, PAD, GROUP)
            dk_acc[pl.ds(first, count), :, lanes] += dk.reshape(count, PAD, GROUP)

    def near(c, r):
        key_side(c, r, r - 1, 3, 0)

    def rim(c, e):
        key_side(c, 7 * e, 1 + 5 * e, 1, 2 - 2 * e)

    sent = []

    def start(copies):
        for copy in copies:
            copy.start()
        sent.extend(copies)

    fill(0)
    pl.semaphore_wait(barrier, len(greeted))
    seam_start(0)
    for copy in lon_copies(0):
        copy.start()
    start([partner_copy(0)])
    fill(1)
    start([partner_copy(1)])
    own(0)
    own(1)
    dk_acc[...] = jnp.zeros_like(dk_acc)
    dv_acc[...] = jnp.zeros_like(dv_acc)
    for load in small:
        load.wait()
    relay_start(0, 0)
    seam_start(1)
    partner_arrive(0)
    partner_arrive(1)
    for copy in lon_copies(0):
        copy.wait_send()
    for copy in lon_rows():
        copy.start()
    relay_start(0, 1)
    for d in range(2):
        lon_arrive(0, d)
    slot_arrive(0, 0, 0)
    slot_arrive(0, 2, 1)

    relay_start(1, 0)

    def query_step(i, carry):
        query_side(i + 1)
        return carry

    lax.fori_loop(0, 6, query_step, 0)
    start([stats_lat(0), stats_lat(1), stats_lon(0), stats_lon(1), result_copy(0)])

    def own_step(i, carry):
        near(1, i + 1)
        return carry

    lax.fori_loop(0, 6, own_step, 0)
    for e in range(2):
        arrive(stats.at[1, 7 * e], 22 + e)
        start([stats_corner(0, e), stats_corner(1, e)])
    relay_start(1, 1)

    def rim_step(e, carry):
        rim(1, e)
        return carry

    lax.fori_loop(0, 2, rim_step, 0)
    mine_lanes = pl.ds(pl.multiple_of(core * HALF, HALF), HALF)
    other_lanes = pl.ds(pl.multiple_of(other * HALF, HALF), HALF)
    stores = [pltpu.make_async_copy(made.at[n], out, lsem.at[7 + n])
              for n, out in enumerate((o_out, dq_out, dk_out, dv_out))]

    def write(i):
        arrive(landed.at[pl.ds(2 * i, 2)], 30 + i)
        for n in (2 * i, 2 * i + 1):
            for r in range(3):
                made[n, r, :, mine_lanes] = result[n, 3 * core + r, 0:TILE, :]
                made[n, r, :, other_lanes] = landed[n, r, 0:TILE, :]
            stores[n].start()

    write(0)
    for d in range(2):
        arrive(stats.at[2 * d, pl.ds(1, 6)], 24 + d)

    def side_step(i, carry):
        r, d, s = i // 4, lax.rem(i // 2, 2), lax.rem(i, 2)
        row = 1 + 3 * s + r
        dst = buf.at[1, :, 2 * d, row]
        pltpu.make_async_remote_copy(
            src_ref=dst, dst_ref=dst, send_sem=row_ssem.at[0], recv_sem=row_rsem.at[i],
            device_id=partner, device_id_type=MESH).wait_recv()
        near(2 * d, row)
        return carry

    lax.fori_loop(0, 12, side_step, 0)
    for d in range(2):
        for e in range(2):
            arrive(stats.at[2 * d, 7 * e], 26 + 2 * d + e)
    slot_arrive(1, 0, 0)
    slot_arrive(1, 2, 1)

    def corner_step(i, carry):
        rim(2 * (i // 2), lax.rem(i, 2))
        return carry

    lax.fori_loop(0, 4, corner_step, 0)
    for r in range(6):
        result[2, r] = (dk_acc[r + 1] * SCALE).astype(jnp.bfloat16)
        result[3, r] = dv_acc[r + 1].astype(jnp.bfloat16)
    start([result_copy(1)])
    write(1)
    for copy in sent + lon_rows():
        copy.wait_send()
    for p in range(2):
        seam_sent(p)
        for step in range(2):
            relay_sent(p, step)
    for store in stores:
        store.wait()


def finish(*refs):
    for i in range(4):
        refs[4 + i][...] = refs[i][...]


def on_device(queries, keys, values, cotangent, pair_list, quad_index, quad_table):
    vmem = pl.BlockSpec(memory_space=pltpu.VMEM)
    hbm = pl.BlockSpec(memory_space=pltpu.HBM)
    pairs = pair_list.T
    outs = [jax.ShapeDtypeStruct(queries.shape, jnp.bfloat16)] * 4
    results = pl.pallas_call(
        kernel,
        out_shape=outs,
        in_specs=[hbm] * 7,
        out_specs=[hbm] * 4,
        scratch_shapes=[
            pltpu.VMEM((4,) + queries.shape, jnp.bfloat16),
            pltpu.VMEM((4,) + queries.shape, jnp.bfloat16),
            pltpu.VMEM((2, 2, 2, 3, PAD, HALF), jnp.bfloat16),
            pltpu.VMEM((2, 2, 3, 8, PAD, HALF), jnp.bfloat16),
            pltpu.VMEM((3, 8, 8, 256), jnp.float32),
            pltpu.VMEM((8, PAD, HALF), jnp.float32),
            pltpu.VMEM((8, PAD, HALF), jnp.float32),
            pltpu.VMEM((4, 6, PAD, HALF), jnp.bfloat16),
            pltpu.VMEM((4, 3, PAD, HALF), jnp.bfloat16),
            pltpu.SMEM(pairs.shape, jnp.int32),
            pltpu.SMEM(quad_index.shape, jnp.int32),
            pltpu.SMEM(quad_table.shape, jnp.float32),
            pltpu.SemaphoreType.DMA((11,)),
            pltpu.SemaphoreType.DMA((40,)),
            pltpu.SemaphoreType.DMA((32,)),
            pltpu.SemaphoreType.DMA((12,)),
            pltpu.SemaphoreType.DMA((12,)),
        ],
        compiler_params=pltpu.CompilerParams(
            collective_id=0, has_side_effects=True, vmem_limit_bytes=VMEM_BYTES),
        name="sphere",
    )(queries, keys, values, cotangent, pairs, quad_index, quad_table)
    return tuple(pl.pallas_call(
        finish,
        out_shape=outs,
        in_specs=[vmem] * 4,
        out_specs=[vmem] * 4,
        compiler_params=pltpu.CompilerParams(vmem_limit_bytes=VMEM_BYTES),
        name="finish",
    )(*results))


def solution(mesh):
    grid = P("lat", "lon", None)
    return jax.shard_map(
        on_device, mesh=mesh, in_specs=(grid,) * 4 + (P(),) * 3, out_specs=(grid,) * 4, check_vma=False)
```

```python
import jax
import jax.numpy as jnp
from jax import lax
from jax.experimental import pallas as pl
from jax.experimental.pallas import tpu as pltpu
from jax.sharding import PartitionSpec as P

HEADS = 16
HEAD = 64
TILE = 45
PAD = 48
NPAIR = 9
RUN = 8
VMEM_BYTES = 64 * 2**20 - 2**17
HALF = 512
GROUP = 256
STACK = 4 * PAD
SCALE = HEAD ** (-0.5)
MESH = pl.DeviceIdType.MESH
NT = (((1,), (1,)), ((), ()))


def dot_nt(a, b):
    return lax.dot_general(a, b, NT, preferred_element_type=jnp.float32)


def dot_nn(a, b):
    return jnp.dot(a, b, preferred_element_type=jnp.float32)


def stacked(tile):
    head = lax.broadcasted_iota(jnp.int32, (PAD, GROUP), 1) // HEAD
    return jnp.concatenate([jnp.where(head == h, tile, jnp.zeros_like(tile)) for h in range(4)], axis=0)


def unstacked(blocks):
    head = lax.broadcasted_iota(jnp.int32, (PAD, GROUP), 1) // HEAD
    out = blocks[0:PAD]
    for h in range(1, 4):
        out = jnp.where(head == h, blocks[h * PAD : (h + 1) * PAD], out)
    return out


def kernel(q_in, k_in, v_in, g_in, pair_in, index_in, table_in, o_out, dq_out, dk_out, dv_out,
           made, loaded, stage, buf, stats, dk_acc, dv_acc, result, landed, pair_ref, index_ref, table_ref,
           lsem, ssem, rsem, row_ssem, row_rsem):
    lat_size, lon_size = lax.axis_size("lat"), lax.axis_size("lon")
    lat, lon = lax.axis_index("lat"), lax.axis_index("lon")
    bands = lat_size // 2
    rows = lat_size * 3
    core = lax.rem(lat, 2)
    band = lat // 2
    other = 1 - core
    east = lax.rem(lon + 1, lon_size)
    west = lax.rem(lon + lon_size - 1, lon_size)
    sides = (east, west)
    up = lax.rem(band + 1, bands)
    down = lax.rem(band + bands - 1, bands)
    toward = lax.rem(band + 2 * core - 1 + bands, bands)
    place = lax.rem(lon, RUN)
    partner = (2 * band + other, lon)

    barrier = pltpu.get_barrier_semaphore()
    greeted = [partner]
    greeted += [(2 * band + h, side) for side in sides for h in range(2)]
    greeted += [(2 * b + h, to) for b in (up, down) for to in (west, lon, east) for h in range(2)]
    for device in greeted:
        pl.semaphore_signal(barrier, inc=1, device_id=device, device_id_type=MESH)

    inputs = (k_in, v_in, q_in, g_in)
    loads = [pltpu.make_async_copy(ref, loaded.at[i], lsem.at[i]) for i, ref in enumerate(inputs)]
    small = [pltpu.make_async_copy(src, dst, lsem.at[4 + i]) for i, (src, dst) in enumerate(
        ((pair_in, pair_ref), (index_in, index_ref), (table_in, table_ref)))]
    for load in loads + small:
        load.start()

    mine = 1 + 3 * core

    def fill(pair):
        for a in range(2):
            loads[2 * pair + a].wait()
            for r in range(3):
                for h in range(2):
                    stage[pair, h, a, r, 32:PAD, :] = jnp.zeros((PAD - 32, HALF), jnp.bfloat16)
                    stage[pair, h, a, r, 0:TILE, :] = loaded[2 * pair + a, r, :, h * HALF : (h + 1) * HALF]

    def own(pair):
        for a in range(2):
            for r in range(3):
                buf[pair, a, 1, mine + r] = stage[pair, core, a, r]

    def send(src, dst, s, r, device):
        return pltpu.make_async_remote_copy(
            src_ref=src, dst_ref=dst, send_sem=ssem.at[s], recv_sem=rsem.at[r],
            device_id=device, device_id_type=MESH)

    def arrive(dst, r):
        send(dst, dst, 0, r, partner).wait_recv()

    def partner_copy(p):
        return send(stage.at[p, other], buf.at[p, :, 1, pl.ds(mine, 3)], 15 * p, 11 * p, partner)

    def lon_copies(p):
        return [send(stage.at[p, h], buf.at[p, :, 2 * d, pl.ds(mine, 3)], 15 * p + 1 + 2 * d + h,
                     11 * p + 1 + 2 * d + core, (2 * band + h, sides[d])) for d in range(2) for h in range(2)]

    def lon_rows():
        return [pltpu.make_async_remote_copy(
            src_ref=stage.at[1, h, :, r], dst_ref=buf.at[1, :, 2 * d, mine + r],
            send_sem=row_ssem.at[4 * r + 2 * d + h], recv_sem=row_rsem.at[4 * r + 2 * d + core],
            device_id=(2 * band + h, sides[d]), device_id_type=MESH)
            for r in range(3) for d in range(2) for h in range(2)]

    def slot(p, col, e):
        return buf.at[p, :, col, 7 * e]

    def seam_copies(p, number, col, to):
        return [send(stage.at[p, h, :, 2 * core], slot(p, col, other), 15 * p + number + h,
                     11 * p + 5 + 2 * col + other, (2 * toward + h, to)) for h in range(2)]

    def seam_near(p):
        return seam_copies(p, 5, 2 * core, core * west + other * east)

    def seam_same(p):
        return seam_copies(p, 7, 1, lon)

    def seam_far(p):
        return seam_copies(p, 9, 2 * other, core * east + other * west)

    def relay(p, e, step):
        col = (2 - step, step)[e]
        to = (1 - step, 1 + step)[e]
        return send(slot(p, col, e), slot(p, to, e), 15 * p + 11 + 2 * step + e, 11 * p + 5 + 2 * to + e,
                    (lat, sides[e]))

    same_when = place == (RUN - 1) * other
    far_when = place == (RUN - 1) * core
    relay_when = (place != RUN - 1, place != 0)

    def seam_start(p):
        for copy in seam_near(p):
            copy.start()

        @pl.when(same_when)
        def _():
            for copy in seam_same(p):
                copy.start()

        @pl.when(far_when)
        def _():
            for copy in seam_far(p):
                copy.start()

    def seam_sent(p):
        for copy in seam_near(p):
            copy.wait_send()

        @pl.when(same_when)
        def _():
            for copy in seam_same(p):
                copy.wait_send()

        @pl.when(far_when)
        def _():
            for copy in seam_far(p):
                copy.wait_send()

    def relay_start(p, step):
        for e in range(2):
            slot_arrive(p, ((2, 0), (1, 1))[step][e], e)

            @pl.when(relay_when[e])
            def _():
                relay(p, e, step).start()

    def relay_sent(p, step):
        for e in range(2):

            @pl.when(relay_when[e])
            def _():
                relay(p, e, step).wait_send()

    def slot_arrive(p, col, e):
        arrive(slot(p, col, e), 11 * p + 5 + 2 * col + e)

    def partner_arrive(p):
        arrive(buf.at[p, :, 1, pl.ds(1 + 3 * other, 3)], 11 * p)

    def lon_arrive(p, d):
        for s in range(2):
            arrive(buf.at[p, :, 2 * d, pl.ds(1 + 3 * s, 3)], 11 * p + 1 + 2 * d + s)

    def stats_lat(e):
        return send(stats.at[1, 6 - 5 * e], stats.at[1, 7 * e], 30 + e, 22 + e, (2 * (up, down)[e] + core, lon))

    def stats_lon(d):
        return send(stats.at[1, pl.ds(1, 6)], stats.at[2 * d, pl.ds(1, 6)], 32 + d, 24 + d, (lat, sides[d]))

    def stats_corner(d, e):
        return send(stats.at[1, 7 * e], stats.at[2 * d, 7 * e], 34 + 2 * d + e, 26 + 2 * d + e, (lat, sides[d]))

    def result_copy(i):
        return send(result.at[pl.ds(2 * i, 2), pl.ds(3 * other, 3)], landed.at[pl.ds(2 * i, 2)], 38 + i, 30 + i, partner)

    def global_row(r):
        return lax.rem(6 * band + r - 1 + rows, rows)

    def row_weight(r):
        return table_ref[index_ref[global_row(r)]]

    def listed(r, code):
        hit = pair_ref[0, global_row(r)] == code
        for s in range(1, NPAIR):
            hit = hit | (pair_ref[s, global_row(r)] == code)
        return hit

    def query_side(r):
        at = lax.broadcasted_iota(jnp.int32, (1, 9 * PAD), 1)
        block = at // PAD
        a = lax.rem(block, 3)
        mask = listed(r, 3 * a + block // 3) & (lax.rem(at, PAD) < TILE)
        weight = jnp.where(a == 0, row_weight(r - 1), jnp.where(a == 1, row_weight(r), row_weight(r + 1)))
        eye = (lax.broadcasted_iota(jnp.int32, (STACK, STACK), 0)
               == lax.broadcasted_iota(jnp.int32, (STACK, STACK), 1))
        for g in range(2):
            lanes = slice(g * GROUP, (g + 1) * GROUP)
            keys = jnp.concatenate(
                [buf[0, 0, c, pl.ds(r - 1, 3), :, lanes].reshape(3 * PAD, GROUP) for c in range(3)], axis=0)
            values = jnp.concatenate(
                [buf[0, 1, c, pl.ds(r - 1, 3), :, lanes].reshape(3 * PAD, GROUP) for c in range(3)], axis=0)
            qm = stacked(buf[1, 0, 1, r, :, lanes])
            gm = stacked(buf[1, 1, 1, r, :, lanes])
            scores = jnp.where(mask, dot_nt(qm, keys) * SCALE, -1e30)
            row_max = jnp.max(scores, axis=1, keepdims=True)
            shares = weight * jnp.exp(scores - row_max)
            total = jnp.sum(shares, axis=1, keepdims=True)
            mixed = dot_nn(shares.astype(jnp.bfloat16), values) / total
            attended = unstacked(mixed).astype(jnp.bfloat16)
            attended4 = jnp.concatenate([attended] * 4, axis=0).astype(jnp.float32)
            delta = jnp.sum(gm.astype(jnp.float32) * attended4, axis=1, keepdims=True)
            lse = row_max + jnp.log(total)
            slopes = shares * (1.0 / total) * (dot_nt(gm, values) - delta)
            grad = dot_nn(slopes.astype(jnp.bfloat16), keys) * SCALE
            result[0, r - 1, :, lanes] = attended
            result[1, r - 1, :, lanes] = unstacked(grad).astype(jnp.bfloat16)
            stats[1, r, g : g + 1, 0:STACK] = jnp.sum(jnp.where(eye, lse, 0.0), axis=0, keepdims=True)
            stats[1, r, 2 + g : 3 + g, 0:STACK] = jnp.sum(jnp.where(eye, delta, 0.0), axis=0, keepdims=True)

    def key_side(c, r, first, count, a_first):
        at = lax.broadcasted_iota(jnp.int32, (count * PAD, 1), 0)
        a = a_first + at // PAD
        mask = listed(r, 3 * a + 2 - c) & (lax.rem(at, PAD) < TILE)
        weight = jnp.full((count * PAD, 1), row_weight(first), jnp.float32)
        for i in range(1, count):
            weight = jnp.where(at >= i * PAD, row_weight(first + i), weight)
        for g in range(2):
            lanes = slice(g * GROUP, (g + 1) * GROUP)
            keys = buf[0, 0, 1, pl.ds(first, count), :, lanes].reshape(count * PAD, GROUP)
            values = buf[0, 1, 1, pl.ds(first, count), :, lanes].reshape(count * PAD, GROUP)
            qm = stacked(buf[1, 0, c, r, :, lanes])
            gm = stacked(buf[1, 1, c, r, :, lanes])
            lse = stats[c, r, g : g + 1, 0:STACK]
            delta = stats[c, r, 2 + g : 3 + g, 0:STACK]
            probs = jnp.where(mask, weight * jnp.exp(dot_nt(keys, qm) * SCALE - lse), 0.0)
            slopes = probs * (dot_nt(values, gm) - delta)
            dv = dot_nn(probs.astype(jnp.bfloat16), gm)
            dk = dot_nn(slopes.astype(jnp.bfloat16), qm)
            dv_acc[pl.ds(first, count), :, lanes] += dv.reshape(count, PAD, GROUP)
            dk_acc[pl.ds(first, count), :, lanes] += dk.reshape(count, PAD, GROUP)

    def near(c, r):
        key_side(c, r, r - 1, 3, 0)

    def rim(c, e):
        key_side(c, 7 * e, 1 + 5 * e, 1, 2 - 2 * e)

    sent = []

    def start(copies):
        for copy in copies:
            copy.start()
        sent.extend(copies)

    fill(0)
    pl.semaphore_wait(barrier, len(greeted))
    seam_start(0)
    for copy in lon_copies(0):
        copy.start()
    start([partner_copy(0)])
    fill(1)
    start([partner_copy(1)])
    own(0)
    own(1)
    dk_acc[...] = jnp.zeros_like(dk_acc)
    dv_acc[...] = jnp.zeros_like(dv_acc)
    for load in small:
        load.wait()
    relay_start(0, 0)
    seam_start(1)
    partner_arrive(0)
    partner_arrive(1)
    for copy in lon_copies(0):
        copy.wait_send()
    relay_start(0, 1)
    for copy in lon_rows()[:8]:
        copy.start()
    for d in range(2):
        lon_arrive(0, d)
    slot_arrive(0, 0, 0)
    slot_arrive(0, 2, 1)

    relay_start(1, 0)

    def query_step(i, carry):
        query_side(i + 1)
        return carry

    lax.fori_loop(0, 6, query_step, 0)
    start([stats_lat(0), stats_lat(1), stats_lon(0), stats_lon(1), result_copy(0)])
    for copy in lon_rows()[:4]:
        copy.wait_send()
    for copy in lon_rows()[8:]:
        copy.start()

    def own_step(i, carry):
        near(1, i + 1)
        return carry

    lax.fori_loop(0, 6, own_step, 0)
    for e in range(2):
        arrive(stats.at[1, 7 * e], 22 + e)
        start([stats_corner(0, e), stats_corner(1, e)])
    relay_start(1, 1)

    def rim_step(e, carry):
        rim(1, e)
        return carry

    lax.fori_loop(0, 2, rim_step, 0)
    mine_lanes = pl.ds(pl.multiple_of(core * HALF, HALF), HALF)
    other_lanes = pl.ds(pl.multiple_of(other * HALF, HALF), HALF)
    stores = [pltpu.make_async_copy(made.at[n], out, lsem.at[7 + n])
              for n, out in enumerate((o_out, dq_out, dk_out, dv_out))]

    def write(i):
        arrive(landed.at[pl.ds(2 * i, 2)], 30 + i)
        for n in (2 * i, 2 * i + 1):
            for r in range(3):
                made[n, r, :, mine_lanes] = result[n, 3 * core + r, 0:TILE, :]
                made[n, r, :, other_lanes] = landed[n, r, 0:TILE, :]
            stores[n].start()

    write(0)
    for d in range(2):
        arrive(stats.at[2 * d, pl.ds(1, 6)], 24 + d)

    def side_step(i, carry):
        r, d, s = i // 4, lax.rem(i // 2, 2), lax.rem(i, 2)
        row = 1 + 3 * s + r
        dst = buf.at[1, :, 2 * d, row]
        pltpu.make_async_remote_copy(
            src_ref=dst, dst_ref=dst, send_sem=row_ssem.at[0], recv_sem=row_rsem.at[i],
            device_id=partner, device_id_type=MESH).wait_recv()
        near(2 * d, row)
        return carry

    lax.fori_loop(0, 12, side_step, 0)
    for d in range(2):
        for e in range(2):
            arrive(stats.at[2 * d, 7 * e], 26 + 2 * d + e)
    slot_arrive(1, 0, 0)
    slot_arrive(1, 2, 1)

    def corner_step(i, carry):
        rim(2 * (i // 2), lax.rem(i, 2))
        return carry

    lax.fori_loop(0, 4, corner_step, 0)
    for r in range(6):
        result[2, r] = (dk_acc[r + 1] * SCALE).astype(jnp.bfloat16)
        result[3, r] = dv_acc[r + 1].astype(jnp.bfloat16)
    start([result_copy(1)])
    write(1)
    for copy in sent + lon_rows()[4:]:
        copy.wait_send()
    for p in range(2):
        seam_sent(p)
        for step in range(2):
            relay_sent(p, step)
    for store in stores:
        store.wait()


def finish(*refs):
    for i in range(4):
        refs[4 + i][...] = refs[i][...]


def on_device(queries, keys, values, cotangent, pair_list, quad_index, quad_table):
    vmem = pl.BlockSpec(memory_space=pltpu.VMEM)
    hbm = pl.BlockSpec(memory_space=pltpu.HBM)
    pairs = pair_list.T
    outs = [jax.ShapeDtypeStruct(queries.shape, jnp.bfloat16)] * 4
    results = pl.pallas_call(
        kernel,
        out_shape=outs,
        in_specs=[hbm] * 7,
        out_specs=[hbm] * 4,
        scratch_shapes=[
            pltpu.VMEM((4,) + queries.shape, jnp.bfloat16),
            pltpu.VMEM((4,) + queries.shape, jnp.bfloat16),
            pltpu.VMEM((2, 2, 2, 3, PAD, HALF), jnp.bfloat16),
            pltpu.VMEM((2, 2, 3, 8, PAD, HALF), jnp.bfloat16),
            pltpu.VMEM((3, 8, 8, 256), jnp.float32),
            pltpu.VMEM((8, PAD, HALF), jnp.float32),
            pltpu.VMEM((8, PAD, HALF), jnp.float32),
            pltpu.VMEM((4, 6, PAD, HALF), jnp.bfloat16),
            pltpu.VMEM((4, 3, PAD, HALF), jnp.bfloat16),
            pltpu.SMEM(pairs.shape, jnp.int32),
            pltpu.SMEM(quad_index.shape, jnp.int32),
            pltpu.SMEM(quad_table.shape, jnp.float32),
            pltpu.SemaphoreType.DMA((11,)),
            pltpu.SemaphoreType.DMA((40,)),
            pltpu.SemaphoreType.DMA((32,)),
            pltpu.SemaphoreType.DMA((12,)),
            pltpu.SemaphoreType.DMA((12,)),
        ],
        compiler_params=pltpu.CompilerParams(
            collective_id=0, has_side_effects=True, vmem_limit_bytes=VMEM_BYTES),
        name="sphere",
    )(queries, keys, values, cotangent, pairs, quad_index, quad_table)
    return tuple(pl.pallas_call(
        finish,
        out_shape=outs,
        in_specs=[vmem] * 4,
        out_specs=[vmem] * 4,
        compiler_params=pltpu.CompilerParams(vmem_limit_bytes=VMEM_BYTES),
        name="finish",
    )(*results))


def solution(mesh):
    grid = P("lat", "lon", None)
    return jax.shard_map(
        on_device, mesh=mesh, in_specs=(grid,) * 4 + (P(),) * 3, out_specs=(grid,) * 4, check_vma=False)
```

```python
import jax
import jax.numpy as jnp
from jax import lax
from jax.experimental import pallas as pl
from jax.experimental.pallas import tpu as pltpu
from jax.sharding import PartitionSpec as P

HEADS = 16
HEAD = 64
TILE = 45
PAD = 48
NPAIR = 9
RUN = 8
VMEM_BYTES = 64 * 2**20 - 2**17
HALF = 512
GROUP = 256
STACK = 4 * PAD
SCALE = HEAD ** (-0.5)
MESH = pl.DeviceIdType.MESH
NT = (((1,), (1,)), ((), ()))


def dot_nt(a, b):
    return lax.dot_general(a, b, NT, preferred_element_type=jnp.float32)


def dot_nn(a, b):
    return jnp.dot(a, b, preferred_element_type=jnp.float32)


def stacked(tile):
    head = lax.broadcasted_iota(jnp.int32, (PAD, GROUP), 1) // HEAD
    return jnp.concatenate([jnp.where(head == h, tile, jnp.zeros_like(tile)) for h in range(4)], axis=0)


def unstacked(blocks):
    head = lax.broadcasted_iota(jnp.int32, (PAD, GROUP), 1) // HEAD
    out = blocks[0:PAD]
    for h in range(1, 4):
        out = jnp.where(head == h, blocks[h * PAD : (h + 1) * PAD], out)
    return out


def kernel(q_in, k_in, v_in, g_in, pair_in, index_in, table_in, o_out, dq_out, dk_out, dv_out,
           made, loaded, stage, buf, stats, dk_acc, dv_acc, result, landed, pair_ref, index_ref, table_ref,
           lsem, ssem, rsem, row_ssem, row_rsem):
    lat_size, lon_size = lax.axis_size("lat"), lax.axis_size("lon")
    lat, lon = lax.axis_index("lat"), lax.axis_index("lon")
    bands = lat_size // 2
    rows = lat_size * 3
    core = lax.rem(lat, 2)
    band = lat // 2
    other = 1 - core
    east = lax.rem(lon + 1, lon_size)
    west = lax.rem(lon + lon_size - 1, lon_size)
    sides = (east, west)
    up = lax.rem(band + 1, bands)
    down = lax.rem(band + bands - 1, bands)
    toward = lax.rem(band + 2 * core - 1 + bands, bands)
    place = lax.rem(lon, RUN)
    partner = (2 * band + other, lon)

    barrier = pltpu.get_barrier_semaphore()
    greeted = [partner]
    greeted += [(2 * band + h, side) for side in sides for h in range(2)]
    greeted += [(2 * b + h, to) for b in (up, down) for to in (west, lon, east) for h in range(2)]
    for device in greeted:
        pl.semaphore_signal(barrier, inc=1, device_id=device, device_id_type=MESH)

    inputs = (k_in, v_in, q_in, g_in)
    loads = [pltpu.make_async_copy(ref, loaded.at[i], lsem.at[i]) for i, ref in enumerate(inputs)]
    small = [pltpu.make_async_copy(src, dst, lsem.at[4 + i]) for i, (src, dst) in enumerate(
        ((pair_in, pair_ref), (index_in, index_ref), (table_in, table_ref)))]
    for load in loads + small:
        load.start()

    mine = 1 + 3 * core

    def fill(pair):
        for a in range(2):
            loads[2 * pair + a].wait()
            for r in range(3):
                for h in range(2):
                    stage[pair, h, a, r, 32:PAD, :] = jnp.zeros((PAD - 32, HALF), jnp.bfloat16)
                    stage[pair, h, a, r, 0:TILE, :] = loaded[2 * pair + a, r, :, h * HALF : (h + 1) * HALF]

    def own(pair):
        for a in range(2):
            for r in range(3):
                buf[pair, a, 1, mine + r] = stage[pair, core, a, r]

    def send(src, dst, s, r, device):
        return pltpu.make_async_remote_copy(
            src_ref=src, dst_ref=dst, send_sem=ssem.at[s], recv_sem=rsem.at[r],
            device_id=device, device_id_type=MESH)

    def arrive(dst, r):
        send(dst, dst, 0, r, partner).wait_recv()

    def partner_copy(p):
        return send(stage.at[p, other], buf.at[p, :, 1, pl.ds(mine, 3)], 15 * p, 11 * p, partner)

    def lon_copies(p):
        return [send(stage.at[p, h], buf.at[p, :, 2 * d, pl.ds(mine, 3)], 15 * p + 1 + 2 * d + h,
                     11 * p + 1 + 2 * d + core, (2 * band + h, sides[d])) for d in range(2) for h in range(2)]

    def lon_rows():
        return [pltpu.make_async_remote_copy(
            src_ref=stage.at[1, h, :, r], dst_ref=buf.at[1, :, 2 * d, mine + r],
            send_sem=row_ssem.at[4 * r + 2 * d + h], recv_sem=row_rsem.at[4 * r + 2 * d + core],
            device_id=(2 * band + h, sides[d]), device_id_type=MESH)
            for r in range(3) for d in range(2) for h in range(2)]

    def slot(p, col, e):
        return buf.at[p, :, col, 7 * e]

    def seam_copies(p, number, col, to):
        return [send(stage.at[p, h, :, 2 * core], slot(p, col, other), 15 * p + number + h,
                     11 * p + 5 + 2 * col + other, (2 * toward + h, to)) for h in range(2)]

    def seam_near(p):
        return seam_copies(p, 5, 2 * core, core * west + other * east)

    def seam_same(p):
        return seam_copies(p, 7, 1, lon)

    def seam_far(p):
        return seam_copies(p, 9, 2 * other, core * east + other * west)

    def relay(p, e, step):
        col = (2 - step, step)[e]
        to = (1 - step, 1 + step)[e]
        return send(slot(p, col, e), slot(p, to, e), 15 * p + 11 + 2 * step + e, 11 * p + 5 + 2 * to + e,
                    (lat, sides[e]))

    same_when = place == (RUN - 1) * other
    far_when = place == (RUN - 1) * core
    at_end = (place == RUN - 1, place == 0)
    relay_when = (place != RUN - 1, place != 0)

    def seam_start(p):
        for copy in seam_near(p):
            copy.start()

        @pl.when(same_when)
        def _():
            for copy in seam_same(p):
                copy.start()

        @pl.when(far_when)
        def _():
            for copy in seam_far(p):
                copy.start()

    def seam_sent(p):
        for copy in seam_near(p):
            copy.wait_send()

        @pl.when(same_when)
        def _():
            for copy in seam_same(p):
                copy.wait_send()

        @pl.when(far_when)
        def _():
            for copy in seam_far(p):
                copy.wait_send()

    def relay_start(p, step):
        for e in range(2):
            slot_arrive(p, ((2, 0), (1, 1))[step][e], e)

            @pl.when(relay_when[e])
            def _():
                relay(p, e, step).start()

    def relay_sent(p, step):
        for e in range(2):

            @pl.when(relay_when[e])
            def _():
                relay(p, e, step).wait_send()

    def slot_arrive(p, col, e):
        arrive(slot(p, col, e), 11 * p + 5 + 2 * col + e)

    def partner_arrive(p):
        arrive(buf.at[p, :, 1, pl.ds(1 + 3 * other, 3)], 11 * p)

    def lon_arrive(p, d):
        for s in range(2):
            arrive(buf.at[p, :, 2 * d, pl.ds(1 + 3 * s, 3)], 11 * p + 1 + 2 * d + s)

    def stats_lat(e):
        return send(stats.at[1, 6 - 5 * e], stats.at[1, 7 * e], 30 + e, 22 + e, (2 * (up, down)[e] + core, lon))

    def stats_lon(d):
        return send(stats.at[1, pl.ds(1, 6)], stats.at[2 * d, pl.ds(1, 6)], 32 + d, 24 + d, (lat, sides[d]))

    def stats_corner(d, e):
        return send(stats.at[1, 7 * e], stats.at[2 * d, 7 * e], 34 + 2 * d + e, 26 + 2 * d + e, (lat, sides[d]))

    def result_copy(i):
        return send(result.at[pl.ds(2 * i, 2), pl.ds(3 * other, 3)], landed.at[pl.ds(2 * i, 2)], 38 + i, 30 + i, partner)

    def global_row(r):
        return lax.rem(6 * band + r - 1 + rows, rows)

    def row_weight(r):
        return table_ref[index_ref[global_row(r)]]

    def listed(r, code):
        hit = pair_ref[0, global_row(r)] == code
        for s in range(1, NPAIR):
            hit = hit | (pair_ref[s, global_row(r)] == code)
        return hit

    def query_side(r):
        at = lax.broadcasted_iota(jnp.int32, (1, 9 * PAD), 1)
        block = at // PAD
        a = lax.rem(block, 3)
        mask = listed(r, 3 * a + block // 3) & (lax.rem(at, PAD) < TILE)
        weight = jnp.where(a == 0, row_weight(r - 1), jnp.where(a == 1, row_weight(r), row_weight(r + 1)))
        eye = (lax.broadcasted_iota(jnp.int32, (STACK, STACK), 0)
               == lax.broadcasted_iota(jnp.int32, (STACK, STACK), 1))
        for g in range(2):
            lanes = slice(g * GROUP, (g + 1) * GROUP)
            keys = jnp.concatenate(
                [buf[0, 0, c, pl.ds(r - 1, 3), :, lanes].reshape(3 * PAD, GROUP) for c in range(3)], axis=0)
            values = jnp.concatenate(
                [buf[0, 1, c, pl.ds(r - 1, 3), :, lanes].reshape(3 * PAD, GROUP) for c in range(3)], axis=0)
            qm = stacked(buf[1, 0, 1, r, :, lanes])
            gm = stacked(buf[1, 1, 1, r, :, lanes])
            scores = jnp.where(mask, dot_nt(qm, keys) * SCALE, -1e30)
            row_max = jnp.max(scores, axis=1, keepdims=True)
            shares = weight * jnp.exp(scores - row_max)
            total = jnp.sum(shares, axis=1, keepdims=True)
            mixed = dot_nn(shares.astype(jnp.bfloat16), values) / total
            attended = unstacked(mixed).astype(jnp.bfloat16)
            attended4 = jnp.concatenate([attended] * 4, axis=0).astype(jnp.float32)
            delta = jnp.sum(gm.astype(jnp.float32) * attended4, axis=1, keepdims=True)
            lse = row_max + jnp.log(total)
            slopes = shares * (1.0 / total) * (dot_nt(gm, values) - delta)
            grad = dot_nn(slopes.astype(jnp.bfloat16), keys) * SCALE
            result[0, r - 1, :, lanes] = attended
            result[1, r - 1, :, lanes] = unstacked(grad).astype(jnp.bfloat16)
            stats[1, r, g : g + 1, 0:STACK] = jnp.sum(jnp.where(eye, lse, 0.0), axis=0, keepdims=True)
            stats[1, r, 2 + g : 3 + g, 0:STACK] = jnp.sum(jnp.where(eye, delta, 0.0), axis=0, keepdims=True)

    def key_side(c, r, first, count, a_first):
        at = lax.broadcasted_iota(jnp.int32, (count * PAD, 1), 0)
        a = a_first + at // PAD
        mask = listed(r, 3 * a + 2 - c) & (lax.rem(at, PAD) < TILE)
        weight = jnp.full((count * PAD, 1), row_weight(first), jnp.float32)
        for i in range(1, count):
            weight = jnp.where(at >= i * PAD, row_weight(first + i), weight)
        for g in range(2):
            lanes = slice(g * GROUP, (g + 1) * GROUP)
            keys = buf[0, 0, 1, pl.ds(first, count), :, lanes].reshape(count * PAD, GROUP)
            values = buf[0, 1, 1, pl.ds(first, count), :, lanes].reshape(count * PAD, GROUP)
            qm = stacked(buf[1, 0, c, r, :, lanes])
            gm = stacked(buf[1, 1, c, r, :, lanes])
            lse = stats[c, r, g : g + 1, 0:STACK]
            delta = stats[c, r, 2 + g : 3 + g, 0:STACK]
            probs = jnp.where(mask, weight * jnp.exp(dot_nt(keys, qm) * SCALE - lse), 0.0)
            slopes = probs * (dot_nt(values, gm) - delta)
            dv = dot_nn(probs.astype(jnp.bfloat16), gm)
            dk = dot_nn(slopes.astype(jnp.bfloat16), qm)
            dv_acc[pl.ds(first, count), :, lanes] += dv.reshape(count, PAD, GROUP)
            dk_acc[pl.ds(first, count), :, lanes] += dk.reshape(count, PAD, GROUP)

    def near(c, r):
        key_side(c, r, r - 1, 3, 0)

    def rim(c, e):
        key_side(c, 7 * e, 1 + 5 * e, 1, 2 - 2 * e)

    sent = []

    def start(copies):
        for copy in copies:
            copy.start()
        sent.extend(copies)

    fill(0)
    pl.semaphore_wait(barrier, len(greeted))
    seam_start(0)
    for copy in lon_copies(0):
        copy.start()
    start([partner_copy(0)])
    fill(1)
    start([partner_copy(1)])
    own(0)
    own(1)
    dk_acc[...] = jnp.zeros_like(dk_acc)
    dv_acc[...] = jnp.zeros_like(dv_acc)
    for load in small:
        load.wait()
    relay_start(0, 0)
    seam_start(1)
    partner_arrive(0)
    partner_arrive(1)
    for copy in lon_copies(0):
        copy.wait_send()
    relay_start(0, 1)
    for copy in lon_rows()[:4]:
        copy.start()
    for d in range(2):

        @pl.when(at_end[d])
        def _():
            for copy in lon_rows()[4 + 2 * d : 6 + 2 * d] + lon_rows()[8 + 2 * d : 10 + 2 * d]:
                copy.start()
    for d in range(2):
        lon_arrive(0, d)
    slot_arrive(0, 0, 0)
    slot_arrive(0, 2, 1)

    relay_start(1, 0)

    def query_step(i, carry):
        query_side(i + 1)
        return carry

    lax.fori_loop(0, 6, query_step, 0)
    start([stats_lat(0), stats_lat(1), stats_lon(0), stats_lon(1), result_copy(0)])
    for copy in lon_rows()[:4]:
        copy.wait_send()
    for d in range(2):

        @pl.when(jnp.logical_not(at_end[d]))
        def _():
            for copy in lon_rows()[4 + 2 * d : 6 + 2 * d] + lon_rows()[8 + 2 * d : 10 + 2 * d]:
                copy.start()

    def own_step(i, carry):
        near(1, i + 1)
        return carry

    lax.fori_loop(0, 6, own_step, 0)
    for e in range(2):
        arrive(stats.at[1, 7 * e], 22 + e)
        start([stats_corner(0, e), stats_corner(1, e)])
    relay_start(1, 1)

    def rim_step(e, carry):
        rim(1, e)
        return carry

    lax.fori_loop(0, 2, rim_step, 0)
    mine_lanes = pl.ds(pl.multiple_of(core * HALF, HALF), HALF)
    other_lanes = pl.ds(pl.multiple_of(other * HALF, HALF), HALF)
    stores = [pltpu.make_async_copy(made.at[n], out, lsem.at[7 + n])
              for n, out in enumerate((o_out, dq_out, dk_out, dv_out))]

    def write(i):
        arrive(landed.at[pl.ds(2 * i, 2)], 30 + i)
        for n in (2 * i, 2 * i + 1):
            for r in range(3):
                made[n, r, :, mine_lanes] = result[n, 3 * core + r, 0:TILE, :]
                made[n, r, :, other_lanes] = landed[n, r, 0:TILE, :]
            stores[n].start()

    write(0)
    for d in range(2):
        arrive(stats.at[2 * d, pl.ds(1, 6)], 24 + d)

    def side_step(i, carry):
        r, d, s = i // 4, lax.rem(i // 2, 2), lax.rem(i, 2)
        row = 1 + 3 * s + r
        dst = buf.at[1, :, 2 * d, row]
        pltpu.make_async_remote_copy(
            src_ref=dst, dst_ref=dst, send_sem=row_ssem.at[0], recv_sem=row_rsem.at[i],
            device_id=partner, device_id_type=MESH).wait_recv()
        near(2 * d, row)
        return carry

    lax.fori_loop(0, 12, side_step, 0)
    for d in range(2):
        for e in range(2):
            arrive(stats.at[2 * d, 7 * e], 26 + 2 * d + e)
    slot_arrive(1, 0, 0)
    slot_arrive(1, 2, 1)

    def corner_step(i, carry):
        rim(2 * (i // 2), lax.rem(i, 2))
        return carry

    lax.fori_loop(0, 4, corner_step, 0)
    for r in range(6):
        result[2, r] = (dk_acc[r + 1] * SCALE).astype(jnp.bfloat16)
        result[3, r] = dv_acc[r + 1].astype(jnp.bfloat16)
    start([result_copy(1)])
    write(1)
    for copy in sent + lon_rows()[4:]:
        copy.wait_send()
    for p in range(2):
        seam_sent(p)
        for step in range(2):
            relay_sent(p, step)
    for store in stores:
        store.wait()


def finish(*refs):
    sources, outs, held, sem = refs[:4], refs[4:8], refs[8], refs[9]
    reads = [pltpu.make_async_copy(sources[i], held.at[i], sem.at[0, i]) for i in range(4)]
    writes = [pltpu.make_async_copy(held.at[i], outs[i], sem.at[1, i]) for i in range(4)]
    for read in reads:
        read.start()
    for read, write in zip(reads, writes):
        read.wait()
        write.start()
    for write in writes:
        write.wait()


def on_device(queries, keys, values, cotangent, pair_list, quad_index, quad_table):
    hbm = pl.BlockSpec(memory_space=pltpu.HBM)
    pairs = pair_list.T
    outs = [jax.ShapeDtypeStruct(queries.shape, jnp.bfloat16)] * 4
    results = pl.pallas_call(
        kernel,
        out_shape=outs,
        in_specs=[hbm] * 7,
        out_specs=[hbm] * 4,
        scratch_shapes=[
            pltpu.VMEM((4,) + queries.shape, jnp.bfloat16),
            pltpu.VMEM((4,) + queries.shape, jnp.bfloat16),
            pltpu.VMEM((2, 2, 2, 3, PAD, HALF), jnp.bfloat16),
            pltpu.VMEM((2, 2, 3, 8, PAD, HALF), jnp.bfloat16),
            pltpu.VMEM((3, 8, 8, 256), jnp.float32),
            pltpu.VMEM((8, PAD, HALF), jnp.float32),
            pltpu.VMEM((8, PAD, HALF), jnp.float32),
            pltpu.VMEM((4, 6, PAD, HALF), jnp.bfloat16),
            pltpu.VMEM((4, 3, PAD, HALF), jnp.bfloat16),
            pltpu.SMEM(pairs.shape, jnp.int32),
            pltpu.SMEM(quad_index.shape, jnp.int32),
            pltpu.SMEM(quad_table.shape, jnp.float32),
            pltpu.SemaphoreType.DMA((11,)),
            pltpu.SemaphoreType.DMA((40,)),
            pltpu.SemaphoreType.DMA((32,)),
            pltpu.SemaphoreType.DMA((12,)),
            pltpu.SemaphoreType.DMA((12,)),
        ],
        compiler_params=pltpu.CompilerParams(
            collective_id=0, has_side_effects=True, vmem_limit_bytes=VMEM_BYTES),
        name="sphere",
    )(queries, keys, values, cotangent, pairs, quad_index, quad_table)
    return tuple(pl.pallas_call(
        finish,
        out_shape=outs,
        in_specs=[hbm] * 4,
        out_specs=[hbm] * 4,
        scratch_shapes=[pltpu.VMEM((4,) + queries.shape, jnp.bfloat16), pltpu.SemaphoreType.DMA((2, 4))],
        compiler_params=pltpu.CompilerParams(vmem_limit_bytes=VMEM_BYTES),
        name="finish",
    )(*results))


def solution(mesh):
    grid = P("lat", "lon", None)
    return jax.shard_map(
        on_device, mesh=mesh, in_specs=(grid,) * 4 + (P(),) * 3, out_specs=(grid,) * 4, check_vma=False)
```

```python
import jax
import jax.numpy as jnp
from jax import lax
from jax.experimental import pallas as pl
from jax.experimental.pallas import tpu as pltpu
from jax.sharding import PartitionSpec as P

HEADS = 16
HEAD = 64
TILE = 45
PAD = 48
NPAIR = 9
RUN = 8
VMEM_BYTES = 64 * 2**20 - 2**17
HALF = 512
GROUP = 256
STACK = 4 * PAD
SCALE = HEAD ** (-0.5)
MESH = pl.DeviceIdType.MESH
NT = (((1,), (1,)), ((), ()))


def dot_nt(a, b):
    return lax.dot_general(a, b, NT, preferred_element_type=jnp.float32)


def dot_nn(a, b):
    return jnp.dot(a, b, preferred_element_type=jnp.float32)


def stacked(tile):
    head = lax.broadcasted_iota(jnp.int32, (PAD, GROUP), 1) // HEAD
    return jnp.concatenate([jnp.where(head == h, tile, jnp.zeros_like(tile)) for h in range(4)], axis=0)


def unstacked(blocks):
    head = lax.broadcasted_iota(jnp.int32, (PAD, GROUP), 1) // HEAD
    out = blocks[0:PAD]
    for h in range(1, 4):
        out = jnp.where(head == h, blocks[h * PAD : (h + 1) * PAD], out)
    return out


def kernel(q_in, k_in, v_in, g_in, pair_in, index_in, table_in, o_out, dq_out, dk_out, dv_out,
           made, loaded, stage, buf, stats, dk_acc, dv_acc, result, landed, pair_ref, index_ref, table_ref,
           lsem, ssem, rsem, row_ssem, row_rsem):
    lat_size, lon_size = lax.axis_size("lat"), lax.axis_size("lon")
    lat, lon = lax.axis_index("lat"), lax.axis_index("lon")
    bands = lat_size // 2
    rows = lat_size * 3
    core = lax.rem(lat, 2)
    band = lat // 2
    other = 1 - core
    east = lax.rem(lon + 1, lon_size)
    west = lax.rem(lon + lon_size - 1, lon_size)
    sides = (east, west)
    up = lax.rem(band + 1, bands)
    down = lax.rem(band + bands - 1, bands)
    toward = lax.rem(band + 2 * core - 1 + bands, bands)
    place = lax.rem(lon, RUN)
    partner = (2 * band + other, lon)

    barrier = pltpu.get_barrier_semaphore()
    greeted = [partner]
    greeted += [(2 * band + h, side) for side in sides for h in range(2)]
    greeted += [(2 * b + h, to) for b in (up, down) for to in (west, lon, east) for h in range(2)]
    for device in greeted:
        pl.semaphore_signal(barrier, inc=1, device_id=device, device_id_type=MESH)

    inputs = (k_in, v_in, q_in, g_in)
    loads = [pltpu.make_async_copy(ref, loaded.at[i], lsem.at[i]) for i, ref in enumerate(inputs)]
    small = [pltpu.make_async_copy(src, dst, lsem.at[4 + i]) for i, (src, dst) in enumerate(
        ((pair_in, pair_ref), (index_in, index_ref), (table_in, table_ref)))]
    for load in loads + small:
        load.start()

    mine = 1 + 3 * core

    def fill(pair):
        for a in range(2):
            loads[2 * pair + a].wait()
            for r in range(3):
                for h in range(2):
                    stage[pair, h, a, r, 32:PAD, :] = jnp.zeros((PAD - 32, HALF), jnp.bfloat16)
                    stage[pair, h, a, r, 0:TILE, :] = loaded[2 * pair + a, r, :, h * HALF : (h + 1) * HALF]

    def own(pair):
        for a in range(2):
            for r in range(3):
                buf[pair, a, 1, mine + r] = stage[pair, core, a, r]

    def send(src, dst, s, r, device):
        return pltpu.make_async_remote_copy(
            src_ref=src, dst_ref=dst, send_sem=ssem.at[s], recv_sem=rsem.at[r],
            device_id=device, device_id_type=MESH)

    def arrive(dst, r):
        send(dst, dst, 0, r, partner).wait_recv()

    def partner_copy(p):
        return send(stage.at[p, other], buf.at[p, :, 1, pl.ds(mine, 3)], 15 * p, 11 * p, partner)

    def lon_copies(p):
        return [send(stage.at[p, h], buf.at[p, :, 2 * d, pl.ds(mine, 3)], 15 * p + 1 + 2 * d + h,
                     11 * p + 1 + 2 * d + core, (2 * band + h, sides[d])) for d in range(2) for h in range(2)]

    def lon_rows():
        return [pltpu.make_async_remote_copy(
            src_ref=stage.at[1, h, :, r], dst_ref=buf.at[1, :, 2 * d, mine + r],
            send_sem=row_ssem.at[4 * r + 2 * d + h], recv_sem=row_rsem.at[4 * r + 2 * d + core],
            device_id=(2 * band + h, sides[d]), device_id_type=MESH)
            for r in range(3) for d in range(2) for h in range(2)]

    def slot(p, col, e):
        return buf.at[p, :, col, 7 * e]

    def seam_copies(p, number, col, to):
        return [send(stage.at[p, h, :, 2 * core], slot(p, col, other), 15 * p + number + h,
                     11 * p + 5 + 2 * col + other, (2 * toward + h, to)) for h in range(2)]

    def seam_near(p):
        return seam_copies(p, 5, 2 * core, core * west + other * east)

    def seam_same(p):
        return seam_copies(p, 7, 1, lon)

    def seam_far(p):
        return seam_copies(p, 9, 2 * other, core * east + other * west)

    def relay(p, e, step):
        col = (2 - step, step)[e]
        to = (1 - step, 1 + step)[e]
        return send(slot(p, col, e), slot(p, to, e), 15 * p + 11 + 2 * step + e, 11 * p + 5 + 2 * to + e,
                    (lat, sides[e]))

    same_when = place == (RUN - 1) * other
    far_when = place == (RUN - 1) * core
    at_end = (place == RUN - 1, place == 0)
    relay_when = (place != RUN - 1, place != 0)

    def seam_start(p):
        for copy in seam_near(p):
            copy.start()

        @pl.when(same_when)
        def _():
            for copy in seam_same(p):
                copy.start()

        @pl.when(far_when)
        def _():
            for copy in seam_far(p):
                copy.start()

    def seam_sent(p):
        for copy in seam_near(p):
            copy.wait_send()

        @pl.when(same_when)
        def _():
            for copy in seam_same(p):
                copy.wait_send()

        @pl.when(far_when)
        def _():
            for copy in seam_far(p):
                copy.wait_send()

    def relay_start(p, step):
        for e in range(2):
            slot_arrive(p, ((2, 0), (1, 1))[step][e], e)

            @pl.when(relay_when[e])
            def _():
                relay(p, e, step).start()

    def relay_sent(p, step):
        for e in range(2):

            @pl.when(relay_when[e])
            def _():
                relay(p, e, step).wait_send()

    def slot_arrive(p, col, e):
        arrive(slot(p, col, e), 11 * p + 5 + 2 * col + e)

    def partner_arrive(p):
        arrive(buf.at[p, :, 1, pl.ds(1 + 3 * other, 3)], 11 * p)

    def lon_arrive(p, d):
        for s in range(2):
            arrive(buf.at[p, :, 2 * d, pl.ds(1 + 3 * s, 3)], 11 * p + 1 + 2 * d + s)

    def stats_lat(e):
        return send(stats.at[1, 6 - 5 * e], stats.at[1, 7 * e], 30 + e, 22 + e, (2 * (up, down)[e] + core, lon))

    def stats_lon(d):
        return send(stats.at[1, pl.ds(1, 6)], stats.at[2 * d, pl.ds(1, 6)], 32 + d, 24 + d, (lat, sides[d]))

    def stats_corner(d, e):
        return send(stats.at[1, 7 * e], stats.at[2 * d, 7 * e], 34 + 2 * d + e, 26 + 2 * d + e, (lat, sides[d]))

    def result_copy(i):
        return send(result.at[pl.ds(2 * i, 2), pl.ds(3 * other, 3)], landed.at[pl.ds(2 * i, 2)], 38 + i, 30 + i, partner)

    def global_row(r):
        return lax.rem(6 * band + r - 1 + rows, rows)

    def row_weight(r):
        return table_ref[index_ref[global_row(r)]]

    def listed(r, code):
        hit = pair_ref[0, global_row(r)] == code
        for s in range(1, NPAIR):
            hit = hit | (pair_ref[s, global_row(r)] == code)
        return hit

    def query_side(r):
        at = lax.broadcasted_iota(jnp.int32, (1, 9 * PAD), 1)
        block = at // PAD
        a = lax.rem(block, 3)
        mask = listed(r, 3 * a + block // 3) & (lax.rem(at, PAD) < TILE)
        weight = jnp.where(a == 0, row_weight(r - 1), jnp.where(a == 1, row_weight(r), row_weight(r + 1)))
        eye = (lax.broadcasted_iota(jnp.int32, (STACK, STACK), 0)
               == lax.broadcasted_iota(jnp.int32, (STACK, STACK), 1))
        for g in range(2):
            lanes = slice(g * GROUP, (g + 1) * GROUP)
            keys = jnp.concatenate(
                [buf[0, 0, c, pl.ds(r - 1, 3), :, lanes].reshape(3 * PAD, GROUP) for c in range(3)], axis=0)
            values = jnp.concatenate(
                [buf[0, 1, c, pl.ds(r - 1, 3), :, lanes].reshape(3 * PAD, GROUP) for c in range(3)], axis=0)
            qm = stacked(buf[1, 0, 1, r, :, lanes])
            gm = stacked(buf[1, 1, 1, r, :, lanes])
            scores = jnp.where(mask, dot_nt(qm, keys) * SCALE, -1e30)
            row_max = jnp.max(scores, axis=1, keepdims=True)
            shares = weight * jnp.exp(scores - row_max)
            total = jnp.sum(shares, axis=1, keepdims=True)
            mixed = dot_nn(shares.astype(jnp.bfloat16), values) / total
            attended = unstacked(mixed).astype(jnp.bfloat16)
            attended4 = jnp.concatenate([attended] * 4, axis=0).astype(jnp.float32)
            delta = jnp.sum(gm.astype(jnp.float32) * attended4, axis=1, keepdims=True)
            lse = row_max + jnp.log(total)
            slopes = shares * (1.0 / total) * (dot_nt(gm, values) - delta)
            grad = dot_nn(slopes.astype(jnp.bfloat16), keys) * SCALE
            result[0, r - 1, :, lanes] = attended
            result[1, r - 1, :, lanes] = unstacked(grad).astype(jnp.bfloat16)
            stats[1, r, g : g + 1, 0:STACK] = jnp.sum(jnp.where(eye, lse, 0.0), axis=0, keepdims=True)
            stats[1, r, 2 + g : 3 + g, 0:STACK] = jnp.sum(jnp.where(eye, delta, 0.0), axis=0, keepdims=True)

    def key_side(c, r, first, count, a_first):
        at = lax.broadcasted_iota(jnp.int32, (count * PAD, 1), 0)
        a = a_first + at // PAD
        mask = listed(r, 3 * a + 2 - c) & (lax.rem(at, PAD) < TILE)
        weight = jnp.full((count * PAD, 1), row_weight(first), jnp.float32)
        for i in range(1, count):
            weight = jnp.where(at >= i * PAD, row_weight(first + i), weight)
        for g in range(2):
            lanes = slice(g * GROUP, (g + 1) * GROUP)
            keys = buf[0, 0, 1, pl.ds(first, count), :, lanes].reshape(count * PAD, GROUP)
            values = buf[0, 1, 1, pl.ds(first, count), :, lanes].reshape(count * PAD, GROUP)
            qm = stacked(buf[1, 0, c, r, :, lanes])
            gm = stacked(buf[1, 1, c, r, :, lanes])
            lse = stats[c, r, g : g + 1, 0:STACK]
            delta = stats[c, r, 2 + g : 3 + g, 0:STACK]
            probs = jnp.where(mask, weight * jnp.exp(dot_nt(keys, qm) * SCALE - lse), 0.0)
            slopes = probs * (dot_nt(values, gm) - delta)
            dv = dot_nn(probs.astype(jnp.bfloat16), gm)
            dk = dot_nn(slopes.astype(jnp.bfloat16), qm)
            dv_acc[pl.ds(first, count), :, lanes] += dv.reshape(count, PAD, GROUP)
            dk_acc[pl.ds(first, count), :, lanes] += dk.reshape(count, PAD, GROUP)

    def near(c, r):
        key_side(c, r, r - 1, 3, 0)

    def rim(c, e):
        key_side(c, 7 * e, 1 + 5 * e, 1, 2 - 2 * e)

    sent = []

    def start(copies):
        for copy in copies:
            copy.start()
        sent.extend(copies)

    fill(0)
    pl.semaphore_wait(barrier, len(greeted))
    seam_start(0)
    for d in range(2):

        @pl.when(at_end[d])
        def _():
            for copy in lon_copies(0)[2 * d : 2 * d + 2]:
                copy.start()

    start([partner_copy(0)])
    fill(1)
    start([partner_copy(1)])
    own(0)
    own(1)
    dk_acc[...] = jnp.zeros_like(dk_acc)
    dv_acc[...] = jnp.zeros_like(dv_acc)
    for load in small:
        load.wait()
    for d in range(2):

        @pl.when(jnp.logical_not(at_end[d]))
        def _():
            for copy in lon_copies(0)[2 * d : 2 * d + 2]:
                copy.start()

    relay_start(0, 0)
    seam_start(1)
    partner_arrive(0)
    partner_arrive(1)
    for copy in lon_copies(0):
        copy.wait_send()
    relay_start(0, 1)
    for copy in lon_rows()[:4]:
        copy.start()
    for d in range(2):

        @pl.when(at_end[d])
        def _():
            for copy in lon_rows()[4 + 2 * d : 6 + 2 * d] + lon_rows()[8 + 2 * d : 10 + 2 * d]:
                copy.start()
    for d in range(2):
        lon_arrive(0, d)
    slot_arrive(0, 0, 0)
    slot_arrive(0, 2, 1)

    relay_start(1, 0)

    def query_step(i, carry):
        query_side(i + 1)
        return carry

    lax.fori_loop(0, 6, query_step, 0)
    start([stats_lat(0), stats_lat(1), stats_lon(0), stats_lon(1), result_copy(0)])
    for copy in lon_rows()[:4]:
        copy.wait_send()
    for d in range(2):

        @pl.when(jnp.logical_not(at_end[d]))
        def _():
            for copy in lon_rows()[4 + 2 * d : 6 + 2 * d] + lon_rows()[8 + 2 * d : 10 + 2 * d]:
                copy.start()

    def own_step(i, carry):
        near(1, i + 1)
        return carry

    lax.fori_loop(0, 6, own_step, 0)
    for e in range(2):
        arrive(stats.at[1, 7 * e], 22 + e)
        start([stats_corner(0, e), stats_corner(1, e)])
    relay_start(1, 1)

    def rim_step(e, carry):
        rim(1, e)
        return carry

    lax.fori_loop(0, 2, rim_step, 0)
    mine_lanes = pl.ds(pl.multiple_of(core * HALF, HALF), HALF)
    other_lanes = pl.ds(pl.multiple_of(other * HALF, HALF), HALF)
    stores = [pltpu.make_async_copy(made.at[n], out, lsem.at[7 + n])
              for n, out in enumerate((o_out, dq_out, dk_out, dv_out))]

    def write(i):
        for n in (2 * i, 2 * i + 1):
            for r in range(3):
                made[n, r, :, mine_lanes] = result[n, 3 * core + r, 0:TILE, :]
        arrive(landed.at[pl.ds(2 * i, 2)], 30 + i)
        for n in (2 * i, 2 * i + 1):
            for r in range(3):
                made[n, r, :, other_lanes] = landed[n, r, 0:TILE, :]
            stores[n].start()

    write(0)
    for d in range(2):
        arrive(stats.at[2 * d, pl.ds(1, 6)], 24 + d)

    def side_step(i, carry):
        r, d, s = i // 4, lax.rem(i // 2, 2), lax.rem(i, 2)
        row = 1 + 3 * s + r
        dst = buf.at[1, :, 2 * d, row]
        pltpu.make_async_remote_copy(
            src_ref=dst, dst_ref=dst, send_sem=row_ssem.at[0], recv_sem=row_rsem.at[i],
            device_id=partner, device_id_type=MESH).wait_recv()
        near(2 * d, row)
        return carry

    lax.fori_loop(0, 12, side_step, 0)
    for d in range(2):
        for e in range(2):
            arrive(stats.at[2 * d, 7 * e], 26 + 2 * d + e)
    slot_arrive(1, 0, 0)
    slot_arrive(1, 2, 1)

    def corner_step(i, carry):
        rim(2 * (i // 2), lax.rem(i, 2))
        return carry

    lax.fori_loop(0, 4, corner_step, 0)
    def round_rows(first):
        for r in range(3):
            result[2, first + r] = (dk_acc[first + r + 1] * SCALE).astype(jnp.bfloat16)
            result[3, first + r] = dv_acc[first + r + 1].astype(jnp.bfloat16)

    round_rows(3 * other)
    start([result_copy(1)])
    round_rows(3 * core)
    write(1)
    for copy in sent + lon_rows()[4:]:
        copy.wait_send()
    for p in range(2):
        seam_sent(p)
        for step in range(2):
            relay_sent(p, step)
    for store in stores:
        store.wait()


def finish(*refs):
    sources, outs, held, sem = refs[:4], refs[4:8], refs[8], refs[9]
    reads = [pltpu.make_async_copy(sources[i], held.at[i], sem.at[0, i]) for i in range(4)]
    writes = [pltpu.make_async_copy(held.at[i], outs[i], sem.at[1, i]) for i in range(4)]
    for read in reads:
        read.start()
    for read, write in zip(reads, writes):
        read.wait()
        write.start()
    for write in writes:
        write.wait()


def on_device(queries, keys, values, cotangent, pair_list, quad_index, quad_table):
    hbm = pl.BlockSpec(memory_space=pltpu.HBM)
    pairs = pair_list.T
    outs = [jax.ShapeDtypeStruct(queries.shape, jnp.bfloat16)] * 4
    results = pl.pallas_call(
        kernel,
        out_shape=outs,
        in_specs=[hbm] * 7,
        out_specs=[hbm] * 4,
        scratch_shapes=[
            pltpu.VMEM((4,) + queries.shape, jnp.bfloat16),
            pltpu.VMEM((4,) + queries.shape, jnp.bfloat16),
            pltpu.VMEM((2, 2, 2, 3, PAD, HALF), jnp.bfloat16),
            pltpu.VMEM((2, 2, 3, 8, PAD, HALF), jnp.bfloat16),
            pltpu.VMEM((3, 8, 8, 256), jnp.float32),
            pltpu.VMEM((8, PAD, HALF), jnp.float32),
            pltpu.VMEM((8, PAD, HALF), jnp.float32),
            pltpu.VMEM((4, 6, PAD, HALF), jnp.bfloat16),
            pltpu.VMEM((4, 3, PAD, HALF), jnp.bfloat16),
            pltpu.SMEM(pairs.shape, jnp.int32),
            pltpu.SMEM(quad_index.shape, jnp.int32),
            pltpu.SMEM(quad_table.shape, jnp.float32),
            pltpu.SemaphoreType.DMA((11,)),
            pltpu.SemaphoreType.DMA((40,)),
            pltpu.SemaphoreType.DMA((32,)),
            pltpu.SemaphoreType.DMA((12,)),
            pltpu.SemaphoreType.DMA((12,)),
        ],
        compiler_params=pltpu.CompilerParams(
            collective_id=0, has_side_effects=True, vmem_limit_bytes=VMEM_BYTES),
        name="sphere",
    )(queries, keys, values, cotangent, pairs, quad_index, quad_table)
    return tuple(pl.pallas_call(
        finish,
        out_shape=outs,
        in_specs=[hbm] * 4,
        out_specs=[hbm] * 4,
        scratch_shapes=[pltpu.VMEM((4,) + queries.shape, jnp.bfloat16), pltpu.SemaphoreType.DMA((2, 4))],
        compiler_params=pltpu.CompilerParams(vmem_limit_bytes=VMEM_BYTES),
        name="finish",
    )(*results))


def solution(mesh):
    grid = P("lat", "lon", None)
    return jax.shard_map(
        on_device, mesh=mesh, in_specs=(grid,) * 4 + (P(),) * 3, out_specs=(grid,) * 4, check_vma=False)
```
